256 devices in a mesh: blk: 128 (over z, y, x_hi, core), grp: 2 (over x_lo).
Axes of the slice: x: 4 (x_hi: 2, x_lo: 2; x = x_hi * 2 + x_lo), y: 4, z: 8, core: 2. Of those that a mesh axis runs over, the one named last changes fastest.
Arguments:
- embeddings: bfloat16 [256, 2048, 768], P('blk', 'grp')
- counts: int32 [256], replicated, may hold values from 512 to 2048, as said below
- plan: int32 [128, 2], replicated, may hold values from 0 to 1
Outputs:
- density: float32 [256, 2048], P('blk', 'grp')
The draws below stay inside these ranges and needn't reach their ends.
Inputs may be any that keep to these rules, and one draw needn't show every extreme that they name: `counts`: some block has exactly 2048 valid rows and some exactly 512.
All inputs are finite; a program needn't handle non-finite values.
Results may differ from the reference program's by a relative error of at most 0.0003.
Values may be sent and summed in bfloat16 or wider, within the bound.
A program may use at most 64 MiB of HBM per device.

```python
import jax
import jax.numpy as jnp
from jax import lax

D = 768
ROWS = 2048
BLOCKS_DEV = 2
ROUNDS = 2
BLOCKS = 256
N_BLK = 128


def draw_embeddings(key, part):
    key = jax.random.fold_in(key, 11)
    key_ids, key_protos, key_scales, key_noise = jax.random.split(key, 4)
    proto_ids = jax.random.randint(key_ids, (BLOCKS, ROWS), 0, 64)
    protos = jax.random.normal(key_protos, (64, D), jnp.float32) / jnp.sqrt(jnp.float32(D))
    noise = jax.random.normal(key_noise, (BLOCKS, ROWS, D), jnp.float32) / jnp.sqrt(jnp.float32(D))
    scales = jnp.exp(jax.random.uniform(key_scales, (BLOCKS, ROWS), jnp.float32, jnp.log(0.2), jnp.log(0.8)))
    values = 0.9 * protos[proto_ids] + scales[:, :, None] * noise
    return values.astype(jnp.bfloat16)


def draw_counts(key, part):
    key = jax.random.fold_in(key, 23)
    key_counts, key_order = jax.random.split(key)
    drawn = jax.random.randint(key_counts, (BLOCKS,), ROWS // 4, ROWS + 1)
    order = jax.random.permutation(key_order, BLOCKS)
    drawn = drawn.at[order[0]].set(ROWS)
    drawn = drawn.at[order[1]].set(ROWS // 4)
    return drawn.astype(jnp.int32)


def set_ends(values, own_key, least, largest):
    longest = values.shape.index(max(values.shape))
    spots = []
    for shift in (0, 1):
        where = [jax.random.randint(jax.random.fold_in(own_key, axis), (), 0, length) for axis, length in enumerate(values.shape)]
        where[longest] = (where[longest] + shift) % values.shape[longest]
        spots.append(tuple(where))
    return values.at[spots[0]].set(least).at[spots[1]].set(largest)


def setup_inputs(seed: int = 0) -> dict:
    streams_of = jax.random.split(jax.random.key(seed), 4)
    return {
        "embeddings": draw_embeddings(jax.random.fold_in(streams_of[3], 71), 0),
        "counts": draw_counts(jax.random.fold_in(streams_of[3], 71), 0),
        "plan": set_ends(jax.random.randint(streams_of[2], (N_BLK, ROUNDS), 0, BLOCKS_DEV), jax.random.fold_in(streams_of[2], 1), 0, BLOCKS_DEV - 1).astype(jnp.int32),
    }


kernel_scale = 4.0


def reference(embeddings, counts, plan):
    norms = jnp.einsum("brd,brd->br", embeddings.astype(jnp.float32), embeddings.astype(jnp.float32))
    row_ids = jnp.arange(ROWS, dtype=jnp.int32)
    valid = (row_ids[None, :] < counts[:, None]).astype(jnp.float32)
    density = jnp.zeros((BLOCKS, ROWS), jnp.float32)
    for turn_index in range(ROUNDS):
        offset = turn_index + 1

        def one_pair(totals, member):
            partner = (member - offset) % N_BLK
            home_block = member * BLOCKS_DEV + plan[member, turn_index]
            guest_block = partner * BLOCKS_DEV + plan[partner, turn_index]
            inner = lax.dot_general(embeddings[home_block], embeddings[guest_block], (((1,), (1,)), ((), ())), preferred_element_type=jnp.float32)
            exponent = norms[home_block][:, None] + norms[guest_block][None, :] - 2.0 * inner
            tile = jnp.exp(-kernel_scale * exponent) * valid[home_block][:, None] * valid[guest_block][None, :]
            totals = totals.at[home_block].add(jnp.sum(tile, axis=1))
            totals = totals.at[guest_block].add(jnp.sum(tile, axis=0))
            return totals, None

        density, _ = lax.scan(one_pair, density, jnp.arange(N_BLK, dtype=jnp.int32))
    return density * valid
```

```python
import functools

import jax
import jax.numpy as jnp
from jax import lax
from jax.experimental import pallas as pl
from jax.experimental.pallas import tpu as pltpu
from jax.sharding import PartitionSpec as P

kernel_scale = 4.0
chunk = 128
mesh_id = pl.DeviceIdType.MESH


def lane_norms(rows, first_row, count):
    wide = rows.astype(jnp.float32)
    squares = wide * wide
    folded = squares[:, :128]
    for start in range(128, rows.shape[1], 128):
        folded = folded + squares[:, start : start + 128]
    norms = 0.5 * jnp.sum(folded.T, axis=0, keepdims=True)
    row_ids = first_row + lax.broadcasted_iota(jnp.int32, norms.shape, 1)
    return jnp.where(row_ids < count, norms, jnp.inf)


def column_norms(rows, first_row, count):
    wide = rows.astype(jnp.float32)
    norms = 0.5 * jnp.sum(wide * wide, axis=1, keepdims=True)
    row_ids = first_row + lax.broadcasted_iota(jnp.int32, norms.shape, 0)
    return jnp.where(row_ids < count, norms, jnp.inf)


def tile_sums(rows, norms, resident, resident_norms, totals):
    row_part = jnp.zeros((chunk, 128), jnp.float32)
    for start in range(0, resident.shape[0], 256):
        inner = lax.dot_general(
            rows, resident[start : start + 256, :], (((1,), (1,)), ((), ())), preferred_element_type=jnp.float32
        )
        for left in (0, 128):
            place = (start + left) // 128
            half_distance = (norms + resident_norms[place : place + 1, :]) - inner[:, left : left + 128]
            values = jnp.exp((-2.0 * kernel_scale) * half_distance)
            row_part = row_part + values
            totals[:, start + left : start + left + 128] += jnp.sum(values.reshape(chunk // 8, 8, 128), axis=0)
    return jnp.sum(row_part.T, axis=0, keepdims=True)


def folded_rows(totals):
    return jnp.concatenate(
        [jnp.sum(totals[:, k * 128 : (k + 1) * 128], axis=0, keepdims=True) for k in range(totals.shape[1] // 128)], axis=0
    )


def kernel(
    blk_count, plan, counts, embeddings, out,
    staged, played_0, played_1, mate_a, mate_b, guest_a, guest_b, chip_guest,
    norms, totals, sums, arrived,
    staged_sem, send_sem, recv_sem, sum_send_sem, sum_recv_sem,
):
    half_rows = embeddings.shape[1]
    chunks = half_rows // chunk
    m, g = lax.axis_index("blk"), lax.axis_index("grp")
    core = lax.rem(m, 2)
    back_1, back_2 = lax.rem(m + blk_count - 1, blk_count), lax.rem(m + blk_count - 2, blk_count)
    next_1, next_2 = lax.rem(m + 1, blk_count), lax.rem(m + 2, blk_count)
    mate, other_core = (m, 1 - g), (m + 1 - 2 * core, g)

    barrier = pltpu.get_barrier_semaphore()
    for device in (mate, (next_2, 1 - g), (back_2, 1 - g), (next_1, 1 - g), (back_1, 1 - g), other_core):
        pl.semaphore_signal(barrier, inc=1, device_id=device, device_id_type=mesh_id)

    def rows_of(k):
        return pl.ds(pl.multiple_of(k * chunk, chunk), chunk)

    def load(k):
        return pltpu.make_async_copy(embeddings.at[:, rows_of(k)], staged.at[:, rows_of(k)], staged_sem.at[k])

    for k in range(chunks):
        load(k).start()

    def copy(stream, source, target, device):
        def of(k):
            return pltpu.make_async_remote_copy(
                src_ref=source.at[rows_of(k)],
                dst_ref=target.at[rows_of(k)],
                send_sem=send_sem.at[stream, k],
                recv_sem=recv_sem.at[stream, k],
                device_id=device,
                device_id_type=mesh_id,
            )

        return of

    def sum_copy(source, target, device):
        return pltpu.make_async_remote_copy(
            src_ref=sums.at[source],
            dst_ref=arrived.at[target],
            send_sem=sum_send_sem.at[target],
            recv_sem=sum_recv_sem.at[target],
            device_id=device,
            device_id_type=mesh_id,
        )

    slot_0, slot_1 = plan[0, m], plan[1, m]
    count_0, count_1 = counts[2 * m + slot_0], counts[2 * m + slot_1]
    guest_count_0 = counts[2 * back_1 + plan[0, back_1]]
    guest_count_1 = counts[2 * back_2 + plan[1, back_2]]
    own_row, far_row = g * half_rows, (1 - g) * half_rows

    totals[...] = jnp.zeros_like(totals)

    to_mate_a0 = copy(0, played_0, mate_a, mate)
    to_mate_a1 = copy(0, played_1, mate_a, mate)
    to_mate_b = copy(1, played_1, mate_b, mate)
    to_next_a = copy(2, played_1, guest_a, (next_2, 1 - g))
    to_next_b = copy(3, played_0, guest_b, (next_1, 1 - g))
    to_core = copy(4, played_0, chip_guest.at[0], other_core)
    to_core_passed = copy(5, mate_a, chip_guest.at[1], other_core)

    pl.semaphore_wait(barrier, 6)
    for k in range(chunks):
        load(k).wait()
        here = rows_of(k)
        first, second = staged[0, here], staged[1, here]
        played_0[here, :] = jnp.where(slot_0 == 0, first, second)
        played_1[here, :] = jnp.where(slot_1 == 0, first, second)

        @pl.when(core == 0)
        def _():
            to_mate_a0(k).start()
            to_next_a(k).start()
            to_core(k).start()

        @pl.when(core == 1)
        def _():
            to_next_b(k).start()
            to_mate_a1(k).start()

    for k in range(chunks):

        @pl.when(core == 0)
        def _():
            to_mate_b(k).start()

        @pl.when(core == 1)
        def _():
            to_next_a(k).start()

    def own_norms(k, carry):
        here = rows_of(k)
        norms[0, pl.ds(k, 1), :] = lane_norms(played_0[here, :], own_row + k * chunk, count_0)
        norms[1, pl.ds(k, 1), :] = lane_norms(played_1[here, :], own_row + k * chunk, count_1)
        return carry

    lax.fori_loop(0, chunks, own_norms, 0)

    @pl.when(core == 0)
    def _():
        def while_arriving(k, carry):
            here = rows_of(k)
            to_mate_a0(k).wait_recv()
            to_core_passed(k).start()
            norms[2, pl.ds(k, 1), :] = lane_norms(mate_a[here, :], far_row + k * chunk, count_0)
            to_next_b(k).wait_recv()
            rows = guest_b[here, :]
            beside = column_norms(rows, far_row + k * chunk, guest_count_0)
            sums[0, pl.ds(k, 1), :] = tile_sums(rows, beside, played_0, norms.at[0], totals.at[0])
            to_next_a(k).wait_recv()
            rows = guest_a[here, :]
            norms[3, pl.ds(k, 1), :] = lane_norms(rows, far_row + k * chunk, guest_count_1)
            beside = column_norms(rows, far_row + k * chunk, guest_count_1)
            sums[1, pl.ds(k, 1), :] = tile_sums(rows, beside, played_1, norms.at[1], totals.at[1])
            return carry

        lax.fori_loop(0, chunks, while_arriving, 0)

        def round_0(k, carry):
            rows = guest_b[rows_of(k), :]
            beside = column_norms(rows, far_row + k * chunk, guest_count_0)
            sums[0, pl.ds(k, 1), :] += tile_sums(rows, beside, mate_a, norms.at[2], totals.at[2])
            return carry

        lax.fori_loop(0, chunks, round_0, 0)
        sums[2] = folded_rows(totals[2])
        sum_copy(0, 5, (back_1, 1 - g)).start()
        sum_copy(2, 0, mate).start()

        def round_1(k, carry):
            to_mate_b(k).wait_recv()
            rows = mate_b[rows_of(k), :]
            beside = column_norms(rows, far_row + k * chunk, count_1)
            sums[3, pl.ds(k, 1), :] = tile_sums(rows, beside, guest_a, norms.at[3], totals.at[3])
            return carry

        lax.fori_loop(0, chunks, round_1, 0)
        sum_copy(3, 1, mate).start()
        sums[1] += folded_rows(totals[3])
        sum_copy(1, 4, (back_2, 1 - g)).start()

    @pl.when(core == 1)
    def _():
        def near_half(k, carry):
            to_core(k).wait_recv()
            rows = chip_guest[0, rows_of(k), :]
            beside = column_norms(rows, own_row + k * chunk, guest_count_0)
            sums[0, pl.ds(k, 1), :] = tile_sums(rows, beside, played_0, norms.at[0], totals.at[0])
            return carry

        lax.fori_loop(0, chunks, near_half, 0)
        sum_copy(0, 2, other_core).start()

        def far_half(k, carry):
            here = rows_of(k)
            to_mate_a1(k).wait_recv()
            norms[2, pl.ds(k, 1), :] = lane_norms(mate_a[here, :], far_row + k * chunk, count_1)
            to_core_passed(k).wait_recv()
            rows = chip_guest[1, here, :]
            beside = column_norms(rows, far_row + k * chunk, guest_count_0)
            sums[1, pl.ds(k, 1), :] = tile_sums(rows, beside, played_0, norms.at[0], totals.at[0])
            return carry

        lax.fori_loop(0, chunks, far_half, 0)
        sum_copy(1, 3, (back_1, 1 - g)).start()

        def round_1(k, carry):
            to_next_a(k).wait_recv()
            rows = guest_a[rows_of(k), :]
            beside = column_norms(rows, far_row + k * chunk, guest_count_1)
            near = tile_sums(rows, beside, played_1, norms.at[1], totals.at[1])
            sums[2, pl.ds(k, 1), :] = near + tile_sums(rows, beside, mate_a, norms.at[2], totals.at[2])
            return carry

        lax.fori_loop(0, chunks, round_1, 0)
        sum_copy(2, 4, (back_2, 1 - g)).start()
        sums[3] = folded_rows(totals[2])
        sum_copy(3, 1, mate).start()

    def store(density_0, density_1):
        places = lax.broadcasted_iota(jnp.int32, (chunks, 128), 0) * 128 + lax.broadcasted_iota(jnp.int32, (chunks, 128), 1)
        for slot in range(2):
            both = jnp.where(slot_0 == slot, density_0, 0.0) + jnp.where(slot_1 == slot, density_1, 0.0)
            both = jnp.where(own_row + places < counts[2 * m + slot], both, 0.0)
            for k in range(chunks):
                out[slot : slot + 1, k * 128 : (k + 1) * 128] = both[k : k + 1, :]

    mine_0, mine_1 = folded_rows(totals[0]), folded_rows(totals[1])

    @pl.when(core == 0)
    def _():
        for target in (0, 1, 2, 3, 4):
            sum_copy(0, target, mate).wait_recv()
        store(mine_0 + arrived[0] + arrived[2] + arrived[3], mine_1 + arrived[1] + arrived[4])
        for k in range(chunks):
            for sent in (to_mate_a0, to_next_a, to_core, to_mate_b, to_core_passed):
                sent(k).wait_send()
        for source, target in ((0, 5), (2, 0), (3, 1), (1, 4)):
            sum_copy(source, target, mate).wait_send()

    @pl.when(core == 1)
    def _():
        for target in (1, 4, 5):
            sum_copy(0, target, mate).wait_recv()
        store(mine_0 + arrived[5], mine_1 + arrived[1] + arrived[4])
        for k in range(chunks):
            for sent in (to_mate_a1, to_next_a, to_next_b):
                sent(k).wait_send()
        for source, target in ((0, 2), (1, 3), (2, 4), (3, 1)):
            sum_copy(source, target, mate).wait_send()


def on_device(embeddings, counts, plan):
    _, half_rows, width = embeddings.shape
    chunks = half_rows // chunk
    half_block = pltpu.VMEM((half_rows, width), embeddings.dtype)
    two_halves = pltpu.VMEM((2, half_rows, width), embeddings.dtype)
    return pl.pallas_call(
        functools.partial(kernel, lax.axis_size("blk")),
        out_shape=jax.ShapeDtypeStruct((2, half_rows), jnp.float32),
        in_specs=[
            pl.BlockSpec(memory_space=pltpu.SMEM),
            pl.BlockSpec(memory_space=pltpu.SMEM),
            pl.BlockSpec(memory_space=pl.ANY),
        ],
        out_specs=pl.BlockSpec(memory_space=pltpu.VMEM),
        scratch_shapes=[
            two_halves,
            half_block, half_block, half_block, half_block, half_block, half_block,
            two_halves,
            pltpu.VMEM((4, chunks, 128), jnp.float32),
            pltpu.VMEM((4, 8, half_rows), jnp.float32),
            pltpu.VMEM((4, chunks, 128), jnp.float32),
            pltpu.VMEM((6, chunks, 128), jnp.float32),
            pltpu.SemaphoreType.DMA((chunks,)),
            pltpu.SemaphoreType.DMA((6, chunks)),
            pltpu.SemaphoreType.DMA((6, chunks)),
            pltpu.SemaphoreType.DMA((6,)),
            pltpu.SemaphoreType.DMA((6,)),
        ],
        compiler_params=pltpu.CompilerParams(
            collective_id=0, has_side_effects=True, vmem_limit_bytes=56 * 2**20
        ),
    )(plan.T, counts, embeddings)


def solution(mesh):
    return jax.shard_map(
        on_device,
        mesh=mesh,
        in_specs=(P("blk", "grp", None), P(), P()),
        out_specs=P("blk", "grp"),
        check_vma=False,
    )
```

```python
import functools

import jax
import jax.numpy as jnp
from jax import lax
from jax.experimental import pallas as pl
from jax.experimental.pallas import tpu as pltpu
from jax.sharding import PartitionSpec as P

kernel_scale = 4.0
chunk = 128
mesh_id = pl.DeviceIdType.MESH


def lane_norms(rows, first_row, count):
    wide = rows.astype(jnp.float32)
    squares = wide * wide
    folded = squares[:, :128]
    for start in range(128, rows.shape[1], 128):
        folded = folded + squares[:, start : start + 128]
    norms = 0.5 * jnp.sum(folded.T, axis=0, keepdims=True)
    row_ids = first_row + lax.broadcasted_iota(jnp.int32, norms.shape, 1)
    return jnp.where(row_ids < count, norms, jnp.inf)


def column_norms(rows, first_row, count):
    wide = rows.astype(jnp.float32)
    norms = 0.5 * jnp.sum(wide * wide, axis=1, keepdims=True)
    row_ids = first_row + lax.broadcasted_iota(jnp.int32, norms.shape, 0)
    return jnp.where(row_ids < count, norms, jnp.inf)


def tile_sums(rows, norms, resident, resident_norms, totals):
    height, width = rows.shape[0], 256
    row_part = jnp.zeros((height, 128), jnp.float32)
    for start in range(0, resident.shape[0], width):
        inner = lax.dot_general(
            rows, resident[start : start + width, :], (((1,), (1,)), ((), ())), preferred_element_type=jnp.float32
        )
        for left in range(0, width, 128):
            place = (start + left) // 128
            half_distance = (norms + resident_norms[place : place + 1, :]) - inner[:, left : left + 128]
            values = jnp.exp((-2.0 * kernel_scale) * half_distance)
            row_part = row_part + values
            totals[:, start + left : start + left + 128] += jnp.sum(values.reshape(height // 8, 8, 128), axis=0)
    return jnp.sum(row_part.T, axis=0, keepdims=True)


def folded_rows(totals):
    return jnp.concatenate(
        [jnp.sum(totals[:, k * 128 : (k + 1) * 128], axis=0, keepdims=True) for k in range(totals.shape[1] // 128)], axis=0
    )


def kernel(
    blk_count, plan_in_hbm, counts_in_hbm, embeddings, out,
    plan, counts, staged, played_0, played_1, mate_a, mate_b, guest_a, guest_b, chip_guest,
    norms, totals, sums, arrived,
    ready, turn, small_sem, staged_sem, send_sem, recv_sem, sum_send_sem, sum_recv_sem,
):
    half_rows = embeddings.shape[1]
    chunks = half_rows // chunk
    m, g = lax.axis_index("blk"), lax.axis_index("grp")
    core = lax.rem(m, 2)
    back_1, back_2 = lax.rem(m + blk_count - 1, blk_count), lax.rem(m + blk_count - 2, blk_count)
    next_1, next_2 = lax.rem(m + 1, blk_count), lax.rem(m + 2, blk_count)
    mate, other_core = (m, 1 - g), (m + 1 - 2 * core, g)

    barrier = pltpu.get_barrier_semaphore()
    sender = (back_1, lax.rem(1 - g + core, 2))
    for device in (mate, (back_2, 1 - g), sender):
        pl.semaphore_signal(barrier, inc=1, device_id=device, device_id_type=mesh_id)

    def rows_of(k):
        return pl.ds(pl.multiple_of(k * chunk, chunk), chunk)

    def load(k):
        return pltpu.make_async_copy(embeddings.at[:, rows_of(k)], staged.at[:, rows_of(k)], staged_sem.at[k])

    load_plan = pltpu.make_async_copy(plan_in_hbm, plan, small_sem.at[0])
    load_counts = pltpu.make_async_copy(counts_in_hbm, counts, small_sem.at[1])
    load_plan.start()
    load_counts.start()
    for k in range(chunks):
        load(k).start()

    def copy(stream, source, target, device):
        def of(k):
            return pltpu.make_async_remote_copy(
                src_ref=source.at[rows_of(k)],
                dst_ref=target.at[rows_of(k)],
                send_sem=send_sem.at[stream, k],
                recv_sem=recv_sem.at[stream, k],
                device_id=device,
                device_id_type=mesh_id,
            )

        return of

    def sum_copy(source, target, device):
        return pltpu.make_async_remote_copy(
            src_ref=sums.at[source],
            dst_ref=arrived.at[target],
            send_sem=sum_send_sem.at[target],
            recv_sem=sum_recv_sem.at[target],
            device_id=device,
            device_id_type=mesh_id,
        )

    totals[...] = jnp.zeros_like(totals)
    own_row, far_row = g * half_rows, (1 - g) * half_rows

    to_mate_a0 = copy(0, played_0, mate_a, mate)
    to_mate_a1 = copy(0, played_1, mate_a, mate)
    to_mate_b = copy(1, played_1, mate_b, mate)
    to_next_a = copy(2, played_1, guest_a, (next_2, 1 - g))
    to_back_a = copy(2, played_1, guest_a, (back_2, 1 - g))
    to_next_b = copy(3, played_0, guest_b, (next_1, 1 - g))
    to_core = copy(4, played_0, chip_guest.at[0], other_core)
    to_core_passed = copy(5, mate_a, chip_guest.at[1], other_core)

    load_plan.wait()
    load_counts.wait()
    slot_0, slot_1 = plan[0, m], plan[1, m]
    count_0, count_1 = counts[2 * m + slot_0], counts[2 * m + slot_1]
    guest_count_0 = counts[2 * back_1 + plan[0, back_1]]
    guest_1 = lax.rem(m + blk_count + 2 - 4 * core, blk_count)
    guest_count_1 = counts[2 * guest_1 + plan[1, guest_1]]

    pl.semaphore_wait(barrier, 3)

    @pl.when(core == 0)
    def _():
        pl.semaphore_signal(ready, inc=1, device_id=(next_2, 1 - g), device_id_type=mesh_id)

    for k in range(chunks):
        load(k).wait()
        here = rows_of(k)
        first, second = staged[0, here], staged[1, here]
        played_0[here, :] = jnp.where(slot_0 == 0, first, second)
        played_1[here, :] = jnp.where(slot_1 == 0, first, second)

        @pl.when(core == 0)
        def _():
            to_mate_a0(k).start()
            to_core(k).start()

        @pl.when(core == 1)
        def _():
            to_next_b(k).start()

    for k in range(chunks):

        @pl.when(core == 0)
        def _():
            to_mate_b(k).start()

        @pl.when(core == 1)
        def _():
            to_next_a(k).start()

    pair = 2 * chunk
    gate = chunks - 5

    def pair_of(i):
        return pl.ds(pl.multiple_of(i * pair, pair), pair)

    def put_norms(place, source, first, first_row, count, many=2):
        for k in range(many):
            rows = source[rows_of(first + k), :]
            norms[place, pl.ds(first + k, 1), :] = lane_norms(rows, first_row + (first + k) * chunk, count)

    def put_sums(place, first, values):
        for k in range(values.shape[1] // 128):
            sums[place, pl.ds(first + k, 1), :] = values[:, k * 128 : (k + 1) * 128]

    def arrive(stream, first, many=2):
        for k in range(many):
            stream(first + k).wait_recv()

    def own_norms(k, carry):
        put_norms(0, played_0, k, own_row, count_0, 1)
        put_norms(1, played_1, k, own_row, count_1, 1)
        return carry

    lax.fori_loop(0, chunks, own_norms, 0)

    def whole(rows, beside, resident, place):
        return tile_sums(rows, beside, resident, norms.at[place], totals.at[place])

    def store(density_0, density_1):
        places = lax.broadcasted_iota(jnp.int32, (chunks, 128), 0) * 128 + lax.broadcasted_iota(jnp.int32, (chunks, 128), 1)
        for slot in range(2):
            both = jnp.where(slot_0 == slot, density_0, 0.0) + jnp.where(slot_1 == slot, density_1, 0.0)
            both = jnp.where(own_row + places < counts[2 * m + slot], both, 0.0)
            for k in range(chunks):
                out[slot : slot + 1, k * 128 : (k + 1) * 128] = both[k : k + 1, :]

    @pl.when(core == 0)
    def _():
        def guests_of_round_0(i, carry):
            for k in range(2):
                to_mate_a0(2 * i + k).wait_recv()
                to_core_passed(2 * i + k).start()
            arrive(to_next_b, 2 * i)
            put_norms(2, guest_b, 2 * i, far_row, guest_count_0)
            rows = guest_b[pair_of(i), :]
            beside = column_norms(rows, far_row + i * pair, guest_count_0)
            put_sums(0, 2 * i, whole(rows, beside, played_0, 0))
            return carry

        lax.fori_loop(0, chunks // 2, guests_of_round_0, 0)

        def mates_of_round_0(i, carry):
            rows = mate_a[pair_of(i), :]
            beside = column_norms(rows, far_row + i * pair, count_0)
            put_sums(2, 2 * i, whole(rows, beside, guest_b, 2))
            return carry

        lax.fori_loop(0, chunks // 2, mates_of_round_0, 0)
        sums[0] += folded_rows(totals[2])
        sum_copy(0, 5, (back_1, 1 - g)).start()
        sum_copy(2, 0, mate).start()

        def mates_of_round_1(k, carry):
            to_mate_b(k).wait_recv()

            @pl.when(k == gate)
            def _():
                pl.semaphore_signal(turn, inc=1, device_id=other_core, device_id_type=mesh_id)
                pl.semaphore_wait(ready, 1)
                for every in range(chunks):
                    to_back_a(every).start()

            put_norms(3, mate_b, k, far_row, count_1, 1)
            return carry

        lax.fori_loop(0, chunks, mates_of_round_1, 0)

        def guests_of_round_1(first, many):
            arrive(to_back_a, first, many)
            rows = guest_a[pl.ds(pl.multiple_of(first * chunk, chunk), many * chunk), :]
            beside = column_norms(rows, far_row + first * chunk, guest_count_1)
            put_sums(1, first, whole(rows, beside, played_1, 1) + whole(rows, beside, mate_b, 3))

        def two_chunks(i, carry):
            guests_of_round_1(2 * i, 2)
            return carry

        lax.fori_loop(0, chunks // 2 - 1, two_chunks, 0)
        for k in range(chunks):
            for sent in (to_mate_a0, to_core, to_core_passed):
                sent(k).wait_send()
        for target in (0, 2, 3):
            sum_copy(0, target, mate).wait_recv()
        density_0 = folded_rows(totals[0]) + arrived[0] + arrived[2] + arrived[3]
        for k in (chunks - 2, chunks - 1):
            guests_of_round_1(k, 1)
        sum_copy(1, 4, (next_2, 1 - g)).start()
        sums[3] = folded_rows(totals[3])
        sum_copy(3, 1, mate).start()

        density_1 = folded_rows(totals[1])
        for k in range(chunks):
            for sent in (to_back_a, to_mate_b):
                sent(k).wait_send()
        for source, target in ((0, 5), (2, 0), (3, 1), (1, 4)):
            sum_copy(source, target, mate).wait_send()
        for target in (1, 4):
            sum_copy(0, target, mate).wait_recv()
        store(density_0, density_1 + arrived[1] + arrived[4])

    @pl.when(core == 1)
    def _():
        def near_half(i, carry):
            arrive(to_core, 2 * i)
            rows = chip_guest[0, pair_of(i), :]
            beside = column_norms(rows, own_row + i * pair, guest_count_0)
            put_sums(0, 2 * i, whole(rows, beside, played_0, 0))
            return carry

        lax.fori_loop(0, chunks // 2, near_half, 0)
        sum_copy(0, 2, other_core).start()

        def far_half(i, carry):
            arrive(to_core_passed, 2 * i)
            rows = chip_guest[1, pair_of(i), :]
            beside = column_norms(rows, far_row + i * pair, guest_count_0)
            put_sums(1, 2 * i, whole(rows, beside, played_0, 0))
            return carry

        lax.fori_loop(0, chunks // 2, far_half, 0)
        sum_copy(1, 3, (back_1, 1 - g)).start()

        def guests_of_round_1(i, carry):
            @pl.when(i == chunks // 2 - 2)
            def _():
                pl.semaphore_wait(turn, 1)
                for every in range(chunks):
                    to_mate_a1(every).start()

            arrive(to_next_a, 2 * i)
            put_norms(2, guest_a, 2 * i, far_row, guest_count_1)
            rows = guest_a[pair_of(i), :]
            beside = column_norms(rows, far_row + i * pair, guest_count_1)
            put_sums(2, 2 * i, whole(rows, beside, played_1, 1))
            return carry

        lax.fori_loop(0, chunks // 2, guests_of_round_1, 0)

        def mates_of_round_1(first, many):
            arrive(to_mate_a1, first, many)
            rows = mate_a[pl.ds(pl.multiple_of(first * chunk, chunk), many * chunk), :]
            beside = column_norms(rows, far_row + first * chunk, count_1)
            put_sums(3, first, whole(rows, beside, guest_a, 2))

        def two_chunks(i, carry):
            mates_of_round_1(2 * i, 2)
            return carry

        lax.fori_loop(0, chunks // 2 - 1, two_chunks, 0)
        for k in range(chunks):
            for sent in (to_next_a, to_next_b):
                sent(k).wait_send()
        sum_copy(0, 5, mate).wait_recv()
        density_0, density_1 = folded_rows(totals[0]) + arrived[5], folded_rows(totals[1])
        for k in (chunks - 2, chunks - 1):
            mates_of_round_1(k, 1)
        sums[2] += folded_rows(totals[2])
        sum_copy(2, 4, (back_2, 1 - g)).start()
        sum_copy(3, 1, mate).start()
        for k in range(chunks):
            to_mate_a1(k).wait_send()
        for source, target in ((0, 2), (1, 3), (2, 4), (3, 1)):
            sum_copy(source, target, mate).wait_send()
        for target in (1, 4):
            sum_copy(0, target, mate).wait_recv()
        store(density_0, density_1 + arrived[1] + arrived[4])


def on_device(embeddings, counts, plan):
    _, half_rows, width = embeddings.shape
    chunks = half_rows // chunk
    half_block = pltpu.VMEM((half_rows, width), embeddings.dtype)
    two_halves = pltpu.VMEM((2, half_rows, width), embeddings.dtype)
    return pl.pallas_call(
        functools.partial(kernel, lax.axis_size("blk")),
        out_shape=jax.ShapeDtypeStruct((2, half_rows), jnp.float32),
        in_specs=[
            pl.BlockSpec(memory_space=pltpu.HBM),
            pl.BlockSpec(memory_space=pltpu.HBM),
            pl.BlockSpec(memory_space=pltpu.HBM),
        ],
        out_specs=pl.BlockSpec(memory_space=pltpu.VMEM),
        scratch_shapes=[
            pltpu.SMEM(plan.shape[::-1], plan.dtype),
            pltpu.SMEM(counts.shape, counts.dtype),
            two_halves,
            half_block, half_block, half_block, half_block, half_block, half_block,
            two_halves,
            pltpu.VMEM((4, chunks, 128), jnp.float32),
            pltpu.VMEM((4, 8, half_rows), jnp.float32),
            pltpu.VMEM((4, chunks, 128), jnp.float32),
            pltpu.VMEM((6, chunks, 128), jnp.float32),
            pltpu.SemaphoreType.REGULAR,
            pltpu.SemaphoreType.REGULAR,
            pltpu.SemaphoreType.DMA((2,)),
            pltpu.SemaphoreType.DMA((chunks,)),
            pltpu.SemaphoreType.DMA((6, chunks)),
            pltpu.SemaphoreType.DMA((6, chunks)),
            pltpu.SemaphoreType.DMA((6,)),
            pltpu.SemaphoreType.DMA((6,)),
        ],
        compiler_params=pltpu.CompilerParams(
            collective_id=0, has_side_effects=True, vmem_limit_bytes=32 * 2**20
        ),
    )(*(pltpu.with_memory_space_constraint(operand, pltpu.HBM) for operand in (plan.T, counts, embeddings)))


def solution(mesh):
    return jax.shard_map(
        on_device,
        mesh=mesh,
        in_specs=(P("blk", "grp", None), P(), P()),
        out_specs=P("blk", "grp"),
        check_vma=False,
    )
```

```python
import functools

import jax
import jax.numpy as jnp
from jax import lax
from jax.experimental import pallas as pl
from jax.experimental.pallas import tpu as pltpu
from jax.sharding import PartitionSpec as P

kernel_scale = 4.0
chunk = 128
mesh_id = pl.DeviceIdType.MESH


def lane_norms(rows, first_row, count):
    wide = rows.astype(jnp.float32)
    squares = wide * wide
    folded = squares[:, :128]
    for start in range(128, rows.shape[1], 128):
        folded = folded + squares[:, start : start + 128]
    norms = 0.5 * jnp.sum(folded.T, axis=0, keepdims=True)
    row_ids = first_row + lax.broadcasted_iota(jnp.int32, norms.shape, 1)
    return jnp.where(row_ids < count, norms, jnp.inf)


def column_norms(rows, first_row, count):
    wide = rows.astype(jnp.float32)
    norms = 0.5 * jnp.sum(wide * wide, axis=1, keepdims=True)
    row_ids = first_row + lax.broadcasted_iota(jnp.int32, norms.shape, 0)
    return jnp.where(row_ids < count, norms, jnp.inf)


def tile_sums(rows, norms, resident, resident_norms, totals):
    height, width = rows.shape[0], 256
    row_part = jnp.zeros((height, 128), jnp.float32)
    for start in range(0, resident.shape[0], width):
        inner = lax.dot_general(
            rows, resident[start : start + width, :], (((1,), (1,)), ((), ())), preferred_element_type=jnp.float32
        )
        for left in range(0, width, 128):
            place = (start + left) // 128
            half_distance = (norms + resident_norms[place : place + 1, :]) - inner[:, left : left + 128]
            values = jnp.exp((-2.0 * kernel_scale) * half_distance)
            row_part = row_part + values
            totals[:, start + left : start + left + 128] += jnp.sum(values.reshape(height // 8, 8, 128), axis=0)
    return jnp.sum(row_part.T, axis=0, keepdims=True)


def folded_rows(totals):
    return jnp.concatenate(
        [jnp.sum(totals[:, k * 128 : (k + 1) * 128], axis=0, keepdims=True) for k in range(totals.shape[1] // 128)], axis=0
    )


def kernel(
    blk_count, plan_in_hbm, counts_in_hbm, embeddings, out,
    plan, counts, staged, played_0, played_1, mate_a, mate_b, guest_a, guest_b, chip_guest,
    norms, totals, sums, arrived,
    ready, turn, small_sem, staged_sem, send_sem, recv_sem, sum_send_sem, sum_recv_sem,
):
    half_rows = embeddings.shape[1]
    ahead = 3
    chunks = half_rows // chunk
    m, g = lax.axis_index("blk"), lax.axis_index("grp")
    core = lax.rem(m, 2)
    back_1, back_2 = lax.rem(m + blk_count - 1, blk_count), lax.rem(m + blk_count - 2, blk_count)
    next_1, next_2 = lax.rem(m + 1, blk_count), lax.rem(m + 2, blk_count)
    mate, other_core = (m, 1 - g), (m + 1 - 2 * core, g)

    barrier = pltpu.get_barrier_semaphore()
    sender = (back_1, lax.rem(1 - g + core, 2))
    for device in (mate, (back_2, 1 - g), sender):
        pl.semaphore_signal(barrier, inc=1, device_id=device, device_id_type=mesh_id)

    def rows_of(k):
        return pl.ds(pl.multiple_of(k * chunk, chunk), chunk)

    def load(k):
        return pltpu.make_async_copy(embeddings.at[:, rows_of(k)], staged.at[:, rows_of(k)], staged_sem.at[k])

    load_plan = pltpu.make_async_copy(plan_in_hbm, plan, small_sem.at[0])
    load_counts = pltpu.make_async_copy(counts_in_hbm, counts, small_sem.at[1])
    load_plan.start()
    load_counts.start()
    for k in range(chunks):
        load(k).start()

    def copy(stream, source, target, device):
        def of(k):
            return pltpu.make_async_remote_copy(
                src_ref=source.at[rows_of(k)],
                dst_ref=target.at[rows_of(k)],
                send_sem=send_sem.at[stream, k],
                recv_sem=recv_sem.at[stream, k],
                device_id=device,
                device_id_type=mesh_id,
            )

        return of

    def sum_copy(source, target, device):
        return pltpu.make_async_remote_copy(
            src_ref=sums.at[source],
            dst_ref=arrived.at[target],
            send_sem=sum_send_sem.at[target],
            recv_sem=sum_recv_sem.at[target],
            device_id=device,
            device_id_type=mesh_id,
        )

    totals[...] = jnp.zeros_like(totals)
    own_row, far_row = g * half_rows, (1 - g) * half_rows

    to_mate_a0 = copy(0, played_0, mate_a, mate)
    to_mate_a1 = copy(0, played_1, mate_a, mate)
    to_mate_b = copy(1, played_1, mate_b, mate)
    to_next_a = copy(2, played_1, guest_a, (next_2, 1 - g))
    to_back_a = copy(2, played_1, guest_a, (back_2, 1 - g))
    to_next_b = copy(3, played_0, guest_b, (next_1, 1 - g))
    to_core = copy(4, played_0, chip_guest.at[0], other_core)
    to_core_passed = copy(5, mate_a, chip_guest.at[1], other_core)

    load_plan.wait()
    load_counts.wait()
    slot_0, slot_1 = plan[0, m], plan[1, m]
    count_0, count_1 = counts[2 * m + slot_0], counts[2 * m + slot_1]
    guest_count_0 = counts[2 * back_1 + plan[0, back_1]]
    guest_1 = lax.rem(m + blk_count + 2 - 4 * core, blk_count)
    guest_count_1 = counts[2 * guest_1 + plan[1, guest_1]]

    pl.semaphore_wait(barrier, 3)

    @pl.when(core == 0)
    def _():
        pl.semaphore_signal(ready, inc=1, device_id=(next_2, 1 - g), device_id_type=mesh_id)

    for k in range(chunks):
        load(k).wait()
        here = rows_of(k)
        first, second = staged[0, here], staged[1, here]
        played_0[here, :] = jnp.where(slot_0 == 0, first, second)
        played_1[here, :] = jnp.where(slot_1 == 0, first, second)

        @pl.when(core == 0)
        def _():
            to_mate_a0(k).start()
            to_core(k).start()

        @pl.when(core == 1)
        def _():
            to_next_b(k).start()

    for k in range(chunks):

        @pl.when(core == 0)
        def _():
            to_mate_b(k).start()

        @pl.when(core == 1)
        def _():
            to_next_a(k).start()

    @pl.when(core == 0)
    def _():
        pl.semaphore_wait(ready, 1)
        for early in range(ahead):
            to_back_a(early).start()

    pair = 2 * chunk
    gate = chunks - 5

    def pair_of(i):
        return pl.ds(pl.multiple_of(i * pair, pair), pair)

    def put_norms(place, source, first, first_row, count, many=2):
        for k in range(many):
            rows = source[rows_of(first + k), :]
            norms[place, pl.ds(first + k, 1), :] = lane_norms(rows, first_row + (first + k) * chunk, count)

    def put_sums(place, first, values):
        for k in range(values.shape[1] // 128):
            sums[place, pl.ds(first + k, 1), :] = values[:, k * 128 : (k + 1) * 128]

    def arrive(stream, first, many=2):
        for k in range(many):
            stream(first + k).wait_recv()

    def own_norms(k, carry):
        put_norms(0, played_0, k, own_row, count_0, 1)
        put_norms(1, played_1, k, own_row, count_1, 1)
        return carry

    lax.fori_loop(0, chunks, own_norms, 0)

    def whole(rows, beside, resident, place):
        return tile_sums(rows, beside, resident, norms.at[place], totals.at[place])

    def store(density_0, density_1):
        places = lax.broadcasted_iota(jnp.int32, (chunks, 128), 0) * 128 + lax.broadcasted_iota(jnp.int32, (chunks, 128), 1)
        for slot in range(2):
            both = jnp.where(slot_0 == slot, density_0, 0.0) + jnp.where(slot_1 == slot, density_1, 0.0)
            both = jnp.where(own_row + places < counts[2 * m + slot], both, 0.0)
            for k in range(chunks):
                out[slot : slot + 1, k * 128 : (k + 1) * 128] = both[k : k + 1, :]

    @pl.when(core == 0)
    def _():
        def guests_of_round_0(i, carry):
            for k in range(2):
                to_mate_a0(2 * i + k).wait_recv()
                to_core_passed(2 * i + k).start()
            arrive(to_next_b, 2 * i)
            put_norms(2, guest_b, 2 * i, far_row, guest_count_0)
            rows = guest_b[pair_of(i), :]
            beside = column_norms(rows, far_row + i * pair, guest_count_0)
            put_sums(0, 2 * i, whole(rows, beside, played_0, 0))
            return carry

        lax.fori_loop(0, chunks // 2, guests_of_round_0, 0)

        def mates_of_round_0(i, carry):
            rows = mate_a[pair_of(i), :]
            beside = column_norms(rows, far_row + i * pair, count_0)
            put_sums(2, 2 * i, whole(rows, beside, guest_b, 2))
            return carry

        lax.fori_loop(0, chunks // 2, mates_of_round_0, 0)
        sums[0] += folded_rows(totals[2])
        sum_copy(0, 5, (back_1, 1 - g)).start()
        sum_copy(2, 0, mate).start()

        def mates_of_round_1(k, carry):
            to_mate_b(k).wait_recv()

            @pl.when(k == gate)
            def _():
                pl.semaphore_signal(turn, inc=1, device_id=other_core, device_id_type=mesh_id)
                for late in range(ahead, chunks):
                    to_back_a(late).start()

            put_norms(3, mate_b, k, far_row, count_1, 1)
            return carry

        lax.fori_loop(0, chunks, mates_of_round_1, 0)

        def guests_of_round_1(first, many):
            arrive(to_back_a, first, many)
            rows = guest_a[pl.ds(pl.multiple_of(first * chunk, chunk), many * chunk), :]
            beside = column_norms(rows, far_row + first * chunk, guest_count_1)
            put_sums(1, first, whole(rows, beside, played_1, 1) + whole(rows, beside, mate_b, 3))

        def two_chunks(i, carry):
            guests_of_round_1(2 * i, 2)
            return carry

        lax.fori_loop(0, chunks // 2 - 1, two_chunks, 0)
        for k in range(chunks):
            for sent in (to_mate_a0, to_core, to_core_passed):
                sent(k).wait_send()
        for target in (0, 2, 3):
            sum_copy(0, target, mate).wait_recv()
        density_0 = folded_rows(totals[0]) + arrived[0] + arrived[2] + arrived[3]
        for k in (chunks - 2, chunks - 1):
            guests_of_round_1(k, 1)
        sum_copy(1, 4, (next_2, 1 - g)).start()
        sums[3] = folded_rows(totals[3])
        sum_copy(3, 1, mate).start()

        density_1 = folded_rows(totals[1])
        for k in range(chunks):
            for sent in (to_back_a, to_mate_b):
                sent(k).wait_send()
        for source, target in ((0, 5), (2, 0), (3, 1), (1, 4)):
            sum_copy(source, target, mate).wait_send()
        for target in (1, 4):
            sum_copy(0, target, mate).wait_recv()
        store(density_0, density_1 + arrived[1] + arrived[4])

    @pl.when(core == 1)
    def _():
        def near_half(i, carry):
            arrive(to_core, 2 * i)
            rows = chip_guest[0, pair_of(i), :]
            beside = column_norms(rows, own_row + i * pair, guest_count_0)
            put_sums(0, 2 * i, whole(rows, beside, played_0, 0))
            return carry

        lax.fori_loop(0, chunks // 2, near_half, 0)
        sum_copy(0, 2, other_core).start()

        def far_half(i, carry):
            arrive(to_core_passed, 2 * i)
            rows = chip_guest[1, pair_of(i), :]
            beside = column_norms(rows, far_row + i * pair, guest_count_0)
            put_sums(1, 2 * i, whole(rows, beside, played_0, 0))
            return carry

        lax.fori_loop(0, chunks // 2, far_half, 0)
        sum_copy(1, 3, (back_1, 1 - g)).start()

        pl.semaphore_wait(turn, 1)
        for k in range(chunks):
            to_mate_a1(k).start()

        early_rows = half_rows - pair

        def guests_of_round_1(i, carry):
            arrive(to_next_a, 2 * i)
            put_norms(2, guest_a, 2 * i, far_row, guest_count_1)
            rows = guest_a[pair_of(i), :]
            beside = column_norms(rows, far_row + i * pair, guest_count_1)
            put_sums(2, 2 * i, whole(rows, beside, played_1, 1))
            return carry

        lax.fori_loop(0, chunks // 2 - 1, guests_of_round_1, 0)

        def mates_of_round_1(first, many):
            arrive(to_mate_a1, first, many)
            put_norms(3, mate_a, first, far_row, count_1, many)
            rows = mate_a[pl.ds(pl.multiple_of(first * chunk, chunk), many * chunk), :]
            beside = column_norms(rows, far_row + first * chunk, count_1)
            put_sums(3, first, whole(rows, beside, guest_a.at[pl.ds(0, early_rows)], 2))

        def two_chunks(i, carry):
            mates_of_round_1(2 * i, 2)
            return carry

        lax.fori_loop(0, chunks // 2 - 1, two_chunks, 0)
        sum_copy(0, 5, mate).wait_recv()
        density_0 = folded_rows(totals[0]) + arrived[5]
        for k in range(chunks):
            to_next_b(k).wait_send()
        for k in (chunks - 2, chunks - 1):
            mates_of_round_1(k, 1)
        arrive(to_next_a, chunks - 2)
        rows = guest_a[early_rows:half_rows, :]
        beside = column_norms(rows, far_row + early_rows, guest_count_1)
        put_sums(2, chunks - 2, whole(rows, beside, played_1, 1) + whole(rows, beside, mate_a, 3))
        sums[2] += folded_rows(totals[2])
        sum_copy(2, 4, (back_2, 1 - g)).start()
        sums[3] += folded_rows(totals[3])
        sum_copy(3, 1, mate).start()
        density_1 = folded_rows(totals[1])
        for k in range(chunks):
            for sent in (to_next_a, to_mate_a1):
                sent(k).wait_send()
        for source, target in ((0, 2), (1, 3), (2, 4), (3, 1)):
            sum_copy(source, target, mate).wait_send()
        for target in (1, 4):
            sum_copy(0, target, mate).wait_recv()
        store(density_0, density_1 + arrived[1] + arrived[4])


def on_device(embeddings, counts, plan):
    _, half_rows, width = embeddings.shape
    chunks = half_rows // chunk
    half_block = pltpu.VMEM((half_rows, width), embeddings.dtype)
    two_halves = pltpu.VMEM((2, half_rows, width), embeddings.dtype)
    return pl.pallas_call(
        functools.partial(kernel, lax.axis_size("blk")),
        out_shape=jax.ShapeDtypeStruct((2, half_rows), jnp.float32),
        in_specs=[
            pl.BlockSpec(memory_space=pltpu.HBM),
            pl.BlockSpec(memory_space=pltpu.HBM),
            pl.BlockSpec(memory_space=pltpu.HBM),
        ],
        out_specs=pl.BlockSpec(memory_space=pltpu.VMEM),
        scratch_shapes=[
            pltpu.SMEM(plan.shape[::-1], plan.dtype),
            pltpu.SMEM(counts.shape, counts.dtype),
            two_halves,
            half_block, half_block, half_block, half_block, half_block, half_block,
            two_halves,
            pltpu.VMEM((4, chunks, 128), jnp.float32),
            pltpu.VMEM((4, 8, half_rows), jnp.float32),
            pltpu.VMEM((4, chunks, 128), jnp.float32),
            pltpu.VMEM((6, chunks, 128), jnp.float32),
            pltpu.SemaphoreType.REGULAR,
            pltpu.SemaphoreType.REGULAR,
            pltpu.SemaphoreType.DMA((2,)),
            pltpu.SemaphoreType.DMA((chunks,)),
            pltpu.SemaphoreType.DMA((6, chunks)),
            pltpu.SemaphoreType.DMA((6, chunks)),
            pltpu.SemaphoreType.DMA((6,)),
            pltpu.SemaphoreType.DMA((6,)),
        ],
        compiler_params=pltpu.CompilerParams(
            collective_id=0, has_side_effects=True, vmem_limit_bytes=32 * 2**20
        ),
    )(*(pltpu.with_memory_space_constraint(operand, pltpu.HBM) for operand in (plan.T, counts, embeddings)))


def solution(mesh):
    return jax.shard_map(
        on_device,
        mesh=mesh,
        in_specs=(P("blk", "grp", None), P(), P()),
        out_specs=P("blk", "grp"),
        check_vma=False,
    )
```

```python
import functools

import jax
import jax.numpy as jnp
from jax import lax
from jax.experimental import pallas as pl
from jax.experimental.pallas import tpu as pltpu
from jax.sharding import PartitionSpec as P

kernel_scale = 4.0
chunk = 128
mesh_id = pl.DeviceIdType.MESH


def lane_norms(rows, first_row, count):
    wide = rows.astype(jnp.float32)
    squares = wide * wide
    folded = squares[:, :128]
    for start in range(128, rows.shape[1], 128):
        folded = folded + squares[:, start : start + 128]
    norms = 0.5 * jnp.sum(folded.T, axis=0, keepdims=True)
    row_ids = first_row + lax.broadcasted_iota(jnp.int32, norms.shape, 1)
    return jnp.where(row_ids < count, norms, jnp.inf)


def column_norms(rows, first_row, count):
    wide = rows.astype(jnp.float32)
    norms = 0.5 * jnp.sum(wide * wide, axis=1, keepdims=True)
    row_ids = first_row + lax.broadcasted_iota(jnp.int32, norms.shape, 0)
    return jnp.where(row_ids < count, norms, jnp.inf)


def tile_sums(rows, norms, resident, resident_norms, totals, turned=False):
    height, width = rows.shape[0], 256
    row_part = jnp.zeros((height, 128), jnp.float32)
    for start in range(0, resident.shape[1 if turned else 0], width):
        if turned:
            inner = jnp.dot(rows, resident[:, start : start + width], preferred_element_type=jnp.float32)
        else:
            inner = lax.dot_general(
                rows, resident[start : start + width, :], (((1,), (1,)), ((), ())), preferred_element_type=jnp.float32
            )
        for left in range(0, width, 128):
            place = (start + left) // 128
            half_distance = (norms + resident_norms[place : place + 1, :]) - inner[:, left : left + 128]
            values = jnp.exp((-2.0 * kernel_scale) * half_distance)
            row_part = row_part + values
            totals[:, start + left : start + left + 128] += jnp.sum(values.reshape(height // 8, 8, 128), axis=0)
    return jnp.sum(row_part.T, axis=0, keepdims=True)


def folded_rows(totals):
    return jnp.concatenate(
        [jnp.sum(totals[:, k * 128 : (k + 1) * 128], axis=0, keepdims=True) for k in range(totals.shape[1] // 128)], axis=0
    )


def kernel(
    blk_count, plan_in_hbm, counts_in_hbm, embeddings, out,
    plan, counts, staged, played_0, played_1, mate_a, mate_b, guest_a, guest_b, chip_guest, turned_1, turned_mate,
    norms, totals, sums, arrived,
    ready, turn, small_sem, staged_sem, send_sem, recv_sem, sum_send_sem, sum_recv_sem,
):
    half_rows = embeddings.shape[1]
    ahead = 3
    chunks = half_rows // chunk
    m, g = lax.axis_index("blk"), lax.axis_index("grp")
    core = lax.rem(m, 2)
    back_1, back_2 = lax.rem(m + blk_count - 1, blk_count), lax.rem(m + blk_count - 2, blk_count)
    next_1, next_2 = lax.rem(m + 1, blk_count), lax.rem(m + 2, blk_count)
    mate, other_core = (m, 1 - g), (m + 1 - 2 * core, g)

    barrier = pltpu.get_barrier_semaphore()
    sender = (back_1, lax.rem(1 - g + core, 2))
    for device in (mate, (back_2, 1 - g), sender):
        pl.semaphore_signal(barrier, inc=1, device_id=device, device_id_type=mesh_id)

    def rows_of(k):
        return pl.ds(pl.multiple_of(k * chunk, chunk), chunk)

    def load(k):
        return pltpu.make_async_copy(embeddings.at[:, rows_of(k)], staged.at[:, rows_of(k)], staged_sem.at[k])

    load_plan = pltpu.make_async_copy(plan_in_hbm, plan, small_sem.at[0])
    load_counts = pltpu.make_async_copy(counts_in_hbm, counts, small_sem.at[1])
    load_plan.start()
    load_counts.start()
    for k in range(chunks):
        load(k).start()

    def copy(stream, source, target, device):
        def of(k):
            return pltpu.make_async_remote_copy(
                src_ref=source.at[rows_of(k)],
                dst_ref=target.at[rows_of(k)],
                send_sem=send_sem.at[stream, k],
                recv_sem=recv_sem.at[stream, k],
                device_id=device,
                device_id_type=mesh_id,
            )

        return of

    def sum_copy(source, target, device):
        return pltpu.make_async_remote_copy(
            src_ref=sums.at[source],
            dst_ref=arrived.at[target],
            send_sem=sum_send_sem.at[target],
            recv_sem=sum_recv_sem.at[target],
            device_id=device,
            device_id_type=mesh_id,
        )

    totals[...] = jnp.zeros_like(totals)
    own_row, far_row = g * half_rows, (1 - g) * half_rows

    to_mate_a0 = copy(0, played_0, mate_a, mate)
    to_mate_a1 = copy(0, played_1, mate_a, mate)
    to_mate_b = copy(1, played_1, mate_b, mate)
    to_next_a = copy(2, played_1, guest_a, (next_2, 1 - g))
    to_back_a = copy(2, played_1, guest_a, (back_2, 1 - g))
    to_next_b = copy(3, played_0, guest_b, (next_1, 1 - g))
    to_core = copy(4, played_0, chip_guest.at[0], other_core)
    to_core_passed = copy(5, mate_a, chip_guest.at[1], other_core)

    load_plan.wait()
    load_counts.wait()
    slot_0, slot_1 = plan[0, m], plan[1, m]
    count_0, count_1 = counts[2 * m + slot_0], counts[2 * m + slot_1]
    guest_count_0 = counts[2 * back_1 + plan[0, back_1]]
    guest_1 = lax.rem(m + blk_count + 2 - 4 * core, blk_count)
    guest_count_1 = counts[2 * guest_1 + plan[1, guest_1]]

    pl.semaphore_wait(barrier, 3)

    @pl.when(core == 0)
    def _():
        pl.semaphore_signal(ready, inc=1, device_id=(next_2, 1 - g), device_id_type=mesh_id)

    for k in range(chunks):
        load(k).wait()
        here = rows_of(k)
        first, second = staged[0, here], staged[1, here]
        played_0[here, :] = jnp.where(slot_0 == 0, first, second)
        played_1[here, :] = jnp.where(slot_1 == 0, first, second)

        @pl.when(core == 0)
        def _():
            to_mate_a0(k).start()
            to_core(k).start()

        @pl.when(core == 1)
        def _():
            to_next_b(k).start()

    for k in range(chunks):

        @pl.when(core == 0)
        def _():
            to_mate_b(k).start()

        @pl.when(core == 1)
        def _():
            to_next_a(k).start()

    @pl.when(core == 0)
    def _():
        pl.semaphore_wait(ready, 1)
        for early in range(ahead):
            to_back_a(early).start()

    pair = 2 * chunk
    turn_gate, back_gate = chunks - 3, chunks - 5

    def pair_of(i):
        return pl.ds(pl.multiple_of(i * pair, pair), pair)

    def put_norms(place, source, first, first_row, count, many=2):
        for k in range(many):
            rows = source[rows_of(first + k), :]
            norms[place, pl.ds(first + k, 1), :] = lane_norms(rows, first_row + (first + k) * chunk, count)

    def put_sums(place, first, values):
        for k in range(values.shape[1] // 128):
            sums[place, pl.ds(first + k, 1), :] = values[:, k * 128 : (k + 1) * 128]

    def arrive(stream, first, many=2):
        for k in range(many):
            stream(first + k).wait_recv()

    def own_norms(k, carry):
        put_norms(0, played_0, k, own_row, count_0, 1)
        put_norms(1, played_1, k, own_row, count_1, 1)
        turned_1[:, rows_of(k)] = played_1[rows_of(k), :].T
        return carry

    lax.fori_loop(0, chunks, own_norms, 0)

    def whole(rows, beside, resident, place):
        return tile_sums(rows, beside, resident, norms.at[place], totals.at[place])

    def whole_turned(rows, beside, resident, place):
        return tile_sums(rows, beside, resident, norms.at[place], totals.at[place], True)

    def store(density_0, density_1):
        places = lax.broadcasted_iota(jnp.int32, (chunks, 128), 0) * 128 + lax.broadcasted_iota(jnp.int32, (chunks, 128), 1)
        for slot in range(2):
            both = jnp.where(slot_0 == slot, density_0, 0.0) + jnp.where(slot_1 == slot, density_1, 0.0)
            both = jnp.where(own_row + places < counts[2 * m + slot], both, 0.0)
            for k in range(chunks):
                out[slot : slot + 1, k * 128 : (k + 1) * 128] = both[k : k + 1, :]

    @pl.when(core == 0)
    def _():
        def guests_of_round_0(i, carry):
            for k in range(2):
                to_mate_a0(2 * i + k).wait_recv()
                to_core_passed(2 * i + k).start()

            @pl.when(i == chunks // 2 - 1)
            def _():
                to_back_a(ahead).start()

            arrive(to_next_b, 2 * i)
            put_norms(2, guest_b, 2 * i, far_row, guest_count_0)
            rows = guest_b[pair_of(i), :]
            beside = column_norms(rows, far_row + i * pair, guest_count_0)
            put_sums(0, 2 * i, whole(rows, beside, played_0, 0))
            return carry

        lax.fori_loop(0, chunks // 2, guests_of_round_0, 0)

        def mates_of_round_0(i, carry):
            rows = mate_a[pair_of(i), :]
            beside = column_norms(rows, far_row + i * pair, count_0)
            put_sums(2, 2 * i, whole(rows, beside, guest_b, 2))
            return carry

        lax.fori_loop(0, chunks // 2, mates_of_round_0, 0)
        sums[0] += folded_rows(totals[2])
        sum_copy(0, 5, (back_1, 1 - g)).start()
        sum_copy(2, 0, mate).start()

        def mates_of_round_1(k, carry):
            to_mate_b(k).wait_recv()

            @pl.when(k == turn_gate)
            def _():
                pl.semaphore_signal(turn, inc=1, device_id=other_core, device_id_type=mesh_id)

            @pl.when(k == back_gate)
            def _():
                for late in range(ahead + 1, chunks):
                    to_back_a(late).start()

            put_norms(3, mate_b, k, far_row, count_1, 1)
            turned_mate[:, rows_of(k)] = mate_b[rows_of(k), :].T
            return carry

        lax.fori_loop(0, chunks, mates_of_round_1, 0)

        def guests_of_round_1(first, many):
            arrive(to_back_a, first, many)
            rows = guest_a[pl.ds(pl.multiple_of(first * chunk, chunk), many * chunk), :]
            beside = column_norms(rows, far_row + first * chunk, guest_count_1)
            put_sums(1, first, whole_turned(rows, beside, turned_1, 1) + whole_turned(rows, beside, turned_mate, 3))

        def two_chunks(i, carry):
            guests_of_round_1(2 * i, 2)
            return carry

        lax.fori_loop(0, chunks // 2 - 1, two_chunks, 0)
        for k in range(chunks):
            for sent in (to_mate_a0, to_core, to_core_passed):
                sent(k).wait_send()
        for target in (0, 2, 3):
            sum_copy(0, target, mate).wait_recv()
        density_0 = folded_rows(totals[0]) + arrived[0] + arrived[2] + arrived[3]
        for k in (chunks - 2, chunks - 1):
            guests_of_round_1(k, 1)
        sum_copy(1, 4, (next_2, 1 - g)).start()
        sums[3] = folded_rows(totals[3])
        sum_copy(3, 1, mate).start()

        density_1 = folded_rows(totals[1])
        for k in range(chunks):
            for sent in (to_back_a, to_mate_b):
                sent(k).wait_send()
        for source, target in ((0, 5), (2, 0), (3, 1), (1, 4)):
            sum_copy(source, target, mate).wait_send()
        for target in (1, 4):
            sum_copy(0, target, mate).wait_recv()
        store(density_0, density_1 + arrived[1] + arrived[4])

    @pl.when(core == 1)
    def _():
        def near_half(i, carry):
            arrive(to_core, 2 * i)
            rows = chip_guest[0, pair_of(i), :]
            beside = column_norms(rows, own_row + i * pair, guest_count_0)
            put_sums(0, 2 * i, whole(rows, beside, played_0, 0))
            return carry

        lax.fori_loop(0, chunks // 2, near_half, 0)
        sum_copy(0, 2, other_core).start()

        def far_half(i, carry):
            arrive(to_core_passed, 2 * i)
            rows = chip_guest[1, pair_of(i), :]
            beside = column_norms(rows, far_row + i * pair, guest_count_0)
            put_sums(1, 2 * i, whole(rows, beside, played_0, 0))
            return carry

        lax.fori_loop(0, chunks // 2, far_half, 0)
        sum_copy(1, 3, (back_1, 1 - g)).start()

        pl.semaphore_wait(turn, 1)
        for k in range(chunks):
            to_mate_a1(k).start()

        early_rows = half_rows - pair

        def guests_of_round_1(i, carry):
            arrive(to_next_a, 2 * i)
            put_norms(2, guest_a, 2 * i, far_row, guest_count_1)
            rows = guest_a[pair_of(i), :]
            beside = column_norms(rows, far_row + i * pair, guest_count_1)
            put_sums(2, 2 * i, whole(rows, beside, played_1, 1))
            return carry

        lax.fori_loop(0, chunks // 2 - 1, guests_of_round_1, 0)

        def mates_of_round_1(first, many):
            arrive(to_mate_a1, first, many)
            put_norms(3, mate_a, first, far_row, count_1, many)
            for k in range(many):
                turned_mate[:, rows_of(first + k)] = mate_a[rows_of(first + k), :].T
            rows = mate_a[pl.ds(pl.multiple_of(first * chunk, chunk), many * chunk), :]
            beside = column_norms(rows, far_row + first * chunk, count_1)
            put_sums(3, first, whole(rows, beside, guest_a.at[pl.ds(0, early_rows)], 2))

        def two_chunks(i, carry):
            mates_of_round_1(2 * i, 2)
            return carry

        lax.fori_loop(0, chunks // 2 - 1, two_chunks, 0)
        sum_copy(0, 5, mate).wait_recv()
        density_0 = folded_rows(totals[0]) + arrived[5]
        for k in range(chunks):
            to_next_b(k).wait_send()
        mates_of_round_1(chunks - 2, 1)

        def last_guests(k):
            to_next_a(k).wait_recv()
            rows = guest_a[k * chunk : (k + 1) * chunk, :]
            beside = column_norms(rows, far_row + k * chunk, guest_count_1)
            return rows, beside, whole_turned(rows, beside, turned_1, 1)

        rows, beside, near = last_guests(chunks - 2)
        mates_of_round_1(chunks - 1, 1)
        put_sums(2, chunks - 2, near + whole_turned(rows, beside, turned_mate, 3))
        rows, beside, near = last_guests(chunks - 1)
        put_sums(2, chunks - 1, near + whole_turned(rows, beside, turned_mate, 3))
        sums[2] += folded_rows(totals[2])
        sum_copy(2, 4, (back_2, 1 - g)).start()
        sums[3] += folded_rows(totals[3])
        sum_copy(3, 1, mate).start()
        density_1 = folded_rows(totals[1])
        for k in range(chunks):
            for sent in (to_next_a, to_mate_a1):
                sent(k).wait_send()
        for source, target in ((0, 2), (1, 3), (2, 4), (3, 1)):
            sum_copy(source, target, mate).wait_send()
        for target in (1, 4):
            sum_copy(0, target, mate).wait_recv()
        store(density_0, density_1 + arrived[1] + arrived[4])


def on_device(embeddings, counts, plan):
    _, half_rows, width = embeddings.shape
    chunks = half_rows // chunk
    half_block = pltpu.VMEM((half_rows, width), embeddings.dtype)
    turned_block = pltpu.VMEM((width, half_rows), embeddings.dtype)
    two_halves = pltpu.VMEM((2, half_rows, width), embeddings.dtype)
    return pl.pallas_call(
        functools.partial(kernel, lax.axis_size("blk")),
        out_shape=jax.ShapeDtypeStruct((2, half_rows), jnp.float32),
        in_specs=[
            pl.BlockSpec(memory_space=pltpu.HBM),
            pl.BlockSpec(memory_space=pltpu.HBM),
            pl.BlockSpec(memory_space=pltpu.HBM),
        ],
        out_specs=pl.BlockSpec(memory_space=pltpu.VMEM),
        scratch_shapes=[
            pltpu.SMEM(plan.shape[::-1], plan.dtype),
            pltpu.SMEM(counts.shape, counts.dtype),
            two_halves,
            half_block, half_block, half_block, half_block, half_block, half_block,
            two_halves,
            turned_block, turned_block,
            pltpu.VMEM((4, chunks, 128), jnp.float32),
            pltpu.VMEM((4, 8, half_rows), jnp.float32),
            pltpu.VMEM((4, chunks, 128), jnp.float32),
            pltpu.VMEM((6, chunks, 128), jnp.float32),
            pltpu.SemaphoreType.REGULAR,
            pltpu.SemaphoreType.REGULAR,
            pltpu.SemaphoreType.DMA((2,)),
            pltpu.SemaphoreType.DMA((chunks,)),
            pltpu.SemaphoreType.DMA((6, chunks)),
            pltpu.SemaphoreType.DMA((6, chunks)),
            pltpu.SemaphoreType.DMA((6,)),
            pltpu.SemaphoreType.DMA((6,)),
        ],
        compiler_params=pltpu.CompilerParams(
            collective_id=0, has_side_effects=True, vmem_limit_bytes=32 * 2**20
        ),
    )(*(pltpu.with_memory_space_constraint(operand, pltpu.HBM) for operand in (plan.T, counts, embeddings)))


def solution(mesh):
    return jax.shard_map(
        on_device,
        mesh=mesh,
        in_specs=(P("blk", "grp", None), P(), P()),
        out_specs=P("blk", "grp"),
        check_vma=False,
    )
```

```python
import functools

import jax
import jax.numpy as jnp
from jax import lax
from jax.experimental import pallas as pl
from jax.experimental.pallas import tpu as pltpu
from jax.sharding import PartitionSpec as P

kernel_scale = 4.0
chunk = 128
mesh_id = pl.DeviceIdType.MESH


def lane_norms(rows, first_row, count):
    wide = rows.astype(jnp.float32)
    squares = wide * wide
    folded = squares[:, :128]
    for start in range(128, rows.shape[1], 128):
        folded = folded + squares[:, start : start + 128]
    norms = 0.5 * jnp.sum(folded.T, axis=0, keepdims=True)
    row_ids = first_row + lax.broadcasted_iota(jnp.int32, norms.shape, 1)
    return jnp.where(row_ids < count, norms, jnp.inf)


def column_norms(rows, first_row, count):
    wide = rows.astype(jnp.float32)
    norms = 0.5 * jnp.sum(wide * wide, axis=1, keepdims=True)
    row_ids = first_row + lax.broadcasted_iota(jnp.int32, norms.shape, 0)
    return jnp.where(row_ids < count, norms, jnp.inf)


def tile_sums(rows, norms, resident, resident_norms, totals, turned=False):
    height, width = rows.shape[0], 256
    row_part = jnp.zeros((height, 128), jnp.float32)
    for start in range(0, resident.shape[1 if turned else 0], width):
        if turned:
            inner = jnp.dot(rows, resident[:, start : start + width], preferred_element_type=jnp.float32)
        else:
            inner = lax.dot_general(
                rows, resident[start : start + width, :], (((1,), (1,)), ((), ())), preferred_element_type=jnp.float32
            )
        for left in range(0, width, 128):
            place = (start + left) // 128
            half_distance = (norms + resident_norms[place : place + 1, :]) - inner[:, left : left + 128]
            values = jnp.exp((-2.0 * kernel_scale) * half_distance)
            row_part = row_part + values
            totals[:, start + left : start + left + 128] += jnp.sum(values.reshape(height // 8, 8, 128), axis=0)
    return jnp.sum(row_part.T, axis=0, keepdims=True)


def folded_rows(totals):
    return jnp.concatenate(
        [jnp.sum(totals[:, k * 128 : (k + 1) * 128], axis=0, keepdims=True) for k in range(totals.shape[1] // 128)], axis=0
    )


def kernel(
    blk_count, plan_in_hbm, counts_in_hbm, embeddings, out,
    plan, counts, staged, played_0, played_1, mate_a, mate_b, guest_a, guest_b, chip_guest, turned_1, turned_mate, turned_guest,
    norms, totals, sums, arrived,
    ready, turn, small_sem, staged_sem, send_sem, recv_sem, sum_send_sem, sum_recv_sem,
):
    half_rows = embeddings.shape[1]
    ahead = 3
    chunks = half_rows // chunk
    m, g = lax.axis_index("blk"), lax.axis_index("grp")
    core = lax.rem(m, 2)
    back_1, back_2 = lax.rem(m + blk_count - 1, blk_count), lax.rem(m + blk_count - 2, blk_count)
    next_1, next_2 = lax.rem(m + 1, blk_count), lax.rem(m + 2, blk_count)
    mate, other_core = (m, 1 - g), (m + 1 - 2 * core, g)

    barrier = pltpu.get_barrier_semaphore()
    sender = (back_1, lax.rem(1 - g + core, 2))
    for device in (mate, (back_2, 1 - g), sender):
        pl.semaphore_signal(barrier, inc=1, device_id=device, device_id_type=mesh_id)

    def rows_of(k):
        return pl.ds(pl.multiple_of(k * chunk, chunk), chunk)

    def load(k):
        return pltpu.make_async_copy(embeddings.at[:, rows_of(k)], staged.at[:, rows_of(k)], staged_sem.at[k])

    load_plan = pltpu.make_async_copy(plan_in_hbm, plan, small_sem.at[0])
    load_counts = pltpu.make_async_copy(counts_in_hbm, counts, small_sem.at[1])
    load_plan.start()
    load_counts.start()
    for k in range(chunks):
        load(k).start()

    def copy(stream, source, target, device):
        def of(k):
            return pltpu.make_async_remote_copy(
                src_ref=source.at[rows_of(k)],
                dst_ref=target.at[rows_of(k)],
                send_sem=send_sem.at[stream, k],
                recv_sem=recv_sem.at[stream, k],
                device_id=device,
                device_id_type=mesh_id,
            )

        return of

    def sum_copy(source, target, device):
        return pltpu.make_async_remote_copy(
            src_ref=sums.at[source],
            dst_ref=arrived.at[target],
            send_sem=sum_send_sem.at[target],
            recv_sem=sum_recv_sem.at[target],
            device_id=device,
            device_id_type=mesh_id,
        )

    totals[...] = jnp.zeros_like(totals)
    own_row, far_row = g * half_rows, (1 - g) * half_rows

    to_mate_a0 = copy(0, played_0, mate_a, mate)
    to_mate_a1 = copy(0, played_1, mate_a, mate)
    to_mate_b = copy(1, played_1, mate_b, mate)
    to_next_a = copy(2, played_1, guest_a, (next_2, 1 - g))
    to_back_a = copy(2, played_1, guest_a, (back_2, 1 - g))
    to_next_b = copy(3, played_0, guest_b, (next_1, 1 - g))
    to_core = copy(4, played_0, chip_guest.at[0], other_core)
    to_core_passed = copy(5, mate_a, chip_guest.at[1], other_core)

    load_plan.wait()
    load_counts.wait()
    slot_0, slot_1 = plan[0, m], plan[1, m]
    count_0, count_1 = counts[2 * m + slot_0], counts[2 * m + slot_1]
    guest_count_0 = counts[2 * back_1 + plan[0, back_1]]
    guest_1 = lax.rem(m + blk_count + 2 - 4 * core, blk_count)
    guest_count_1 = counts[2 * guest_1 + plan[1, guest_1]]

    pl.semaphore_wait(barrier, 3)

    @pl.when(core == 0)
    def _():
        pl.semaphore_signal(ready, inc=1, device_id=(next_2, 1 - g), device_id_type=mesh_id)

    for k in range(chunks):
        load(k).wait()
        here = rows_of(k)
        first, second = staged[0, here], staged[1, here]
        played_0[here, :] = jnp.where(slot_0 == 0, first, second)
        played_1[here, :] = jnp.where(slot_1 == 0, first, second)

        @pl.when(core == 0)
        def _():
            to_mate_a0(k).start()
            to_core(k).start()

        @pl.when(core == 1)
        def _():
            to_next_b(k).start()

    for k in range(chunks):

        @pl.when(core == 0)
        def _():
            to_mate_b(k).start()

        @pl.when(core == 1)
        def _():
            to_next_a(k).start()

    @pl.when(core == 0)
    def _():
        pl.semaphore_wait(ready, 1)
        for early in range(ahead):
            to_back_a(early).start()

    pair = 2 * chunk
    turn_gate, back_gate = chunks - 3, chunks - 5

    def pair_of(i):
        return pl.ds(pl.multiple_of(i * pair, pair), pair)

    def put_norms(place, source, first, first_row, count, many=2):
        for k in range(many):
            rows = source[rows_of(first + k), :]
            norms[place, pl.ds(first + k, 1), :] = lane_norms(rows, first_row + (first + k) * chunk, count)

    def put_sums(place, first, values):
        for k in range(values.shape[1] // 128):
            sums[place, pl.ds(first + k, 1), :] = values[:, k * 128 : (k + 1) * 128]

    def arrive(stream, first, many=2):
        for k in range(many):
            stream(first + k).wait_recv()

    def own_norms(k, carry):
        put_norms(0, played_0, k, own_row, count_0, 1)
        put_norms(1, played_1, k, own_row, count_1, 1)
        turned_1[:, rows_of(k)] = played_1[rows_of(k), :].T
        return carry

    lax.fori_loop(0, chunks, own_norms, 0)

    def whole(rows, beside, resident, place):
        return tile_sums(rows, beside, resident, norms.at[place], totals.at[place])

    def whole_turned(rows, beside, resident, place):
        return tile_sums(rows, beside, resident, norms.at[place], totals.at[place], True)

    def store(density_0, density_1):
        places = lax.broadcasted_iota(jnp.int32, (chunks, 128), 0) * 128 + lax.broadcasted_iota(jnp.int32, (chunks, 128), 1)
        for slot in range(2):
            both = jnp.where(slot_0 == slot, density_0, 0.0) + jnp.where(slot_1 == slot, density_1, 0.0)
            both = jnp.where(own_row + places < counts[2 * m + slot], both, 0.0)
            for k in range(chunks):
                out[slot : slot + 1, k * 128 : (k + 1) * 128] = both[k : k + 1, :]

    @pl.when(core == 0)
    def _():
        def guests_of_round_0(i, carry):
            for k in range(2):
                to_mate_a0(2 * i + k).wait_recv()
                to_core_passed(2 * i + k).start()

            @pl.when(i == chunks // 2 - 1)
            def _():
                to_back_a(ahead).start()

            arrive(to_next_b, 2 * i)
            put_norms(2, guest_b, 2 * i, far_row, guest_count_0)
            rows = guest_b[pair_of(i), :]
            beside = column_norms(rows, far_row + i * pair, guest_count_0)
            put_sums(0, 2 * i, whole(rows, beside, played_0, 0))
            return carry

        lax.fori_loop(0, chunks // 2, guests_of_round_0, 0)

        def mates_of_round_0(i, carry):
            rows = mate_a[pair_of(i), :]
            beside = column_norms(rows, far_row + i * pair, count_0)
            put_sums(2, 2 * i, whole(rows, beside, guest_b, 2))
            return carry

        lax.fori_loop(0, chunks // 2, mates_of_round_0, 0)
        sums[0] += folded_rows(totals[2])
        sum_copy(0, 5, (back_1, 1 - g)).start()
        sum_copy(2, 0, mate).start()

        def mates_of_round_1(k, carry):
            to_mate_b(k).wait_recv()

            @pl.when(k == turn_gate)
            def _():
                pl.semaphore_signal(turn, inc=1, device_id=other_core, device_id_type=mesh_id)

            @pl.when(k == back_gate)
            def _():
                for late in range(ahead + 1, chunks):
                    to_back_a(late).start()

            put_norms(3, mate_b, k, far_row, count_1, 1)
            turned_mate[:, rows_of(k)] = mate_b[rows_of(k), :].T
            return carry

        lax.fori_loop(0, chunks, mates_of_round_1, 0)

        def guests_of_round_1(first, many):
            arrive(to_back_a, first, many)
            rows = guest_a[pl.ds(pl.multiple_of(first * chunk, chunk), many * chunk), :]
            beside = column_norms(rows, far_row + first * chunk, guest_count_1)
            put_sums(1, first, whole_turned(rows, beside, turned_1, 1) + whole_turned(rows, beside, turned_mate, 3))

        def two_chunks(i, carry):
            guests_of_round_1(2 * i, 2)
            return carry

        lax.fori_loop(0, chunks // 2 - 1, two_chunks, 0)
        for k in range(chunks):
            for sent in (to_mate_a0, to_core, to_core_passed):
                sent(k).wait_send()
        for target in (0, 2, 3):
            sum_copy(0, target, mate).wait_recv()
        density_0 = folded_rows(totals[0]) + arrived[0] + arrived[2] + arrived[3]
        for k in (chunks - 2, chunks - 1):
            guests_of_round_1(k, 1)
        sum_copy(1, 4, (next_2, 1 - g)).start()
        sums[3] = folded_rows(totals[3])
        sum_copy(3, 1, mate).start()

        density_1 = folded_rows(totals[1])
        for k in range(chunks):
            for sent in (to_back_a, to_mate_b):
                sent(k).wait_send()
        for source, target in ((0, 5), (2, 0), (3, 1), (1, 4)):
            sum_copy(source, target, mate).wait_send()
        for target in (1, 4):
            sum_copy(0, target, mate).wait_recv()
        store(density_0, density_1 + arrived[1] + arrived[4])

    @pl.when(core == 1)
    def _():
        def near_half(i, carry):
            arrive(to_core, 2 * i)
            rows = chip_guest[0, pair_of(i), :]
            beside = column_norms(rows, own_row + i * pair, guest_count_0)
            put_sums(0, 2 * i, whole(rows, beside, played_0, 0))
            return carry

        lax.fori_loop(0, chunks // 2, near_half, 0)
        sum_copy(0, 2, other_core).start()

        def far_half(i, carry):
            arrive(to_core_passed, 2 * i)
            rows = chip_guest[1, pair_of(i), :]
            beside = column_norms(rows, far_row + i * pair, guest_count_0)
            put_sums(1, 2 * i, whole(rows, beside, played_0, 0))
            return carry

        lax.fori_loop(0, chunks // 2, far_half, 0)
        sum_copy(1, 3, (back_1, 1 - g)).start()

        pl.semaphore_wait(turn, 1)
        for k in range(chunks):
            to_mate_a1(k).start()

        early_rows = half_rows - pair

        def guests_of_round_1(i, carry):
            arrive(to_next_a, 2 * i)
            put_norms(2, guest_a, 2 * i, far_row, guest_count_1)
            for k in range(2):
                turned_guest[:, rows_of(2 * i + k)] = guest_a[rows_of(2 * i + k), :].T
            rows = guest_a[pair_of(i), :]
            beside = column_norms(rows, far_row + i * pair, guest_count_1)
            put_sums(2, 2 * i, whole(rows, beside, played_1, 1))
            return carry

        lax.fori_loop(0, chunks // 2 - 1, guests_of_round_1, 0)

        def mates_of_round_1(first, many):
            arrive(to_mate_a1, first, many)
            put_norms(3, mate_a, first, far_row, count_1, many)
            for k in range(many):
                turned_mate[:, rows_of(first + k)] = mate_a[rows_of(first + k), :].T
            rows = mate_a[pl.ds(pl.multiple_of(first * chunk, chunk), many * chunk), :]
            beside = column_norms(rows, far_row + first * chunk, count_1)
            put_sums(3, first, whole_turned(rows, beside, turned_guest.at[:, pl.ds(0, early_rows)], 2))

        def two_chunks(i, carry):
            mates_of_round_1(2 * i, 2)
            return carry

        lax.fori_loop(0, chunks // 2 - 1, two_chunks, 0)
        sum_copy(0, 5, mate).wait_recv()
        density_0 = folded_rows(totals[0]) + arrived[5]
        for k in range(chunks):
            to_next_b(k).wait_send()
        mates_of_round_1(chunks - 2, 1)

        def last_guests(k):
            to_next_a(k).wait_recv()
            rows = guest_a[k * chunk : (k + 1) * chunk, :]
            beside = column_norms(rows, far_row + k * chunk, guest_count_1)
            return rows, beside, whole_turned(rows, beside, turned_1, 1)

        rows, beside, near = last_guests(chunks - 2)
        mates_of_round_1(chunks - 1, 1)
        put_sums(2, chunks - 2, near + whole_turned(rows, beside, turned_mate, 3))
        sums[2] += folded_rows(totals[2])
        rows, beside, near = last_guests(chunks - 1)
        put_sums(2, chunks - 1, near + whole_turned(rows, beside, turned_mate, 3))
        sum_copy(2, 4, (back_2, 1 - g)).start()
        sums[3] += folded_rows(totals[3])
        sum_copy(3, 1, mate).start()
        density_1 = folded_rows(totals[1])
        for k in range(chunks):
            for sent in (to_next_a, to_mate_a1):
                sent(k).wait_send()
        for source, target in ((0, 2), (1, 3), (2, 4), (3, 1)):
            sum_copy(source, target, mate).wait_send()
        for target in (1, 4):
            sum_copy(0, target, mate).wait_recv()
        store(density_0, density_1 + arrived[1] + arrived[4])


def on_device(embeddings, counts, plan):
    _, half_rows, width = embeddings.shape
    chunks = half_rows // chunk
    half_block = pltpu.VMEM((half_rows, width), embeddings.dtype)
    turned_block = pltpu.VMEM((width, half_rows), embeddings.dtype)
    two_halves = pltpu.VMEM((2, half_rows, width), embeddings.dtype)
    return pl.pallas_call(
        functools.partial(kernel, lax.axis_size("blk")),
        out_shape=jax.ShapeDtypeStruct((2, half_rows), jnp.float32),
        in_specs=[
            pl.BlockSpec(memory_space=pltpu.HBM),
            pl.BlockSpec(memory_space=pltpu.HBM),
            pl.BlockSpec(memory_space=pltpu.HBM),
        ],
        out_specs=pl.BlockSpec(memory_space=pltpu.VMEM),
        scratch_shapes=[
            pltpu.SMEM(plan.shape[::-1], plan.dtype),
            pltpu.SMEM(counts.shape, counts.dtype),
            two_halves,
            half_block, half_block, half_block, half_block, half_block, half_block,
            two_halves,
            turned_block, turned_block, turned_block,
            pltpu.VMEM((4, chunks, 128), jnp.float32),
            pltpu.VMEM((4, 8, half_rows), jnp.float32),
            pltpu.VMEM((4, chunks, 128), jnp.float32),
            pltpu.VMEM((6, chunks, 128), jnp.float32),
            pltpu.SemaphoreType.REGULAR,
            pltpu.SemaphoreType.REGULAR,
            pltpu.SemaphoreType.DMA((2,)),
            pltpu.SemaphoreType.DMA((chunks,)),
            pltpu.SemaphoreType.DMA((6, chunks)),
            pltpu.SemaphoreType.DMA((6, chunks)),
            pltpu.SemaphoreType.DMA((6,)),
            pltpu.SemaphoreType.DMA((6,)),
        ],
        compiler_params=pltpu.CompilerParams(
            collective_id=0, has_side_effects=True, vmem_limit_bytes=32 * 2**20
        ),
    )(*(pltpu.with_memory_space_constraint(operand, pltpu.HBM) for operand in (plan.T, counts, embeddings)))


def solution(mesh):
    return jax.shard_map(
        on_device,
        mesh=mesh,
        in_specs=(P("blk", "grp", None), P(), P()),
        out_specs=P("blk", "grp"),
        check_vma=False,
    )
```

```python
import functools

import jax
import jax.numpy as jnp
from jax import lax
from jax.experimental import pallas as pl
from jax.experimental.pallas import tpu as pltpu
from jax.sharding import PartitionSpec as P

kernel_scale = 4.0
chunk = 128
mesh_id = pl.DeviceIdType.MESH


def lane_norms(rows, first_row, count):
    wide = rows.astype(jnp.float32)
    squares = wide * wide
    folded = squares[:, :128]
    for start in range(128, rows.shape[1], 128):
        folded = folded + squares[:, start : start + 128]
    norms = 0.5 * jnp.sum(folded.T, axis=0, keepdims=True)
    row_ids = first_row + lax.broadcasted_iota(jnp.int32, norms.shape, 1)
    return jnp.where(row_ids < count, norms, jnp.inf)


def column_norms(rows, first_row, count):
    wide = rows.astype(jnp.float32)
    norms = 0.5 * jnp.sum(wide * wide, axis=1, keepdims=True)
    row_ids = first_row + lax.broadcasted_iota(jnp.int32, norms.shape, 0)
    return jnp.where(row_ids < count, norms, jnp.inf)


def tile_sums(rows, norms, resident, resident_norms, totals, turned=False):
    height, width = rows.shape[0], 256
    row_part = jnp.zeros((height, 128), jnp.float32)
    for start in range(0, resident.shape[1 if turned else 0], width):
        if turned:
            inner = jnp.dot(rows, resident[:, start : start + width], preferred_element_type=jnp.float32)
        else:
            inner = lax.dot_general(
                rows, resident[start : start + width, :], (((1,), (1,)), ((), ())), preferred_element_type=jnp.float32
            )
        for left in range(0, width, 128):
            place = (start + left) // 128
            half_distance = (norms + resident_norms[place : place + 1, :]) - inner[:, left : left + 128]
            values = jnp.exp((-2.0 * kernel_scale) * half_distance)
            row_part = row_part + values
            totals[:, start + left : start + left + 128] += jnp.sum(values.reshape(height // 8, 8, 128), axis=0)
    return jnp.sum(row_part.T, axis=0, keepdims=True)


def folded_rows(totals):
    return jnp.concatenate(
        [jnp.sum(totals[:, k * 128 : (k + 1) * 128], axis=0, keepdims=True) for k in range(totals.shape[1] // 128)], axis=0
    )


def kernel(
    blk_count, plan_in_hbm, counts_in_hbm, embeddings, out,
    plan, counts, staged, played_0, played_1, mate_a, mate_b, guest_a, guest_b, chip_guest, turned_1, turned_mate,
    norms, totals, sums, arrived,
    ready, turn, small_sem, staged_sem, send_sem, recv_sem, sum_send_sem, sum_recv_sem,
):
    half_rows = embeddings.shape[1]
    ahead = 3
    chunks = half_rows // chunk
    m, g = lax.axis_index("blk"), lax.axis_index("grp")
    core = lax.rem(m, 2)
    back_1, back_2 = lax.rem(m + blk_count - 1, blk_count), lax.rem(m + blk_count - 2, blk_count)
    next_1, next_2 = lax.rem(m + 1, blk_count), lax.rem(m + 2, blk_count)
    mate, other_core = (m, 1 - g), (m + 1 - 2 * core, g)

    barrier = pltpu.get_barrier_semaphore()
    sender = (back_1, lax.rem(1 - g + core, 2))
    for device in (mate, (back_2, 1 - g), sender):
        pl.semaphore_signal(barrier, inc=1, device_id=device, device_id_type=mesh_id)

    def rows_of(k):
        return pl.ds(pl.multiple_of(k * chunk, chunk), chunk)

    def load(k):
        return pltpu.make_async_copy(embeddings.at[:, rows_of(k)], staged.at[:, rows_of(k)], staged_sem.at[k])

    load_plan = pltpu.make_async_copy(plan_in_hbm, plan, small_sem.at[0])
    load_counts = pltpu.make_async_copy(counts_in_hbm, counts, small_sem.at[1])
    load_plan.start()
    load_counts.start()
    for k in range(chunks):
        load(k).start()

    def copy(stream, source, target, device):
        def of(k):
            return pltpu.make_async_remote_copy(
                src_ref=source.at[rows_of(k)],
                dst_ref=target.at[rows_of(k)],
                send_sem=send_sem.at[stream, k],
                recv_sem=recv_sem.at[stream, k],
                device_id=device,
                device_id_type=mesh_id,
            )

        return of

    def sum_copy(source, target, device):
        return pltpu.make_async_remote_copy(
            src_ref=sums.at[source],
            dst_ref=arrived.at[target],
            send_sem=sum_send_sem.at[target],
            recv_sem=sum_recv_sem.at[target],
            device_id=device,
            device_id_type=mesh_id,
        )

    totals[...] = jnp.zeros_like(totals)
    own_row, far_row = g * half_rows, (1 - g) * half_rows

    to_mate_a0 = copy(0, played_0, mate_a, mate)
    to_mate_a1 = copy(0, played_1, mate_a, mate)
    to_mate_b = copy(1, played_1, mate_b, mate)
    to_next_a = copy(2, played_1, guest_a, (next_2, 1 - g))
    to_back_a = copy(2, played_1, guest_a, (back_2, 1 - g))
    to_next_b = copy(3, played_0, guest_b, (next_1, 1 - g))
    to_core = copy(4, played_0, chip_guest.at[0], other_core)
    to_core_passed = copy(5, mate_a, chip_guest.at[1], other_core)

    load_plan.wait()
    load_counts.wait()
    slot_0, slot_1 = plan[0, m], plan[1, m]
    count_0, count_1 = counts[2 * m + slot_0], counts[2 * m + slot_1]
    guest_count_0 = counts[2 * back_1 + plan[0, back_1]]
    guest_1 = lax.rem(m + blk_count + 2 - 4 * core, blk_count)
    guest_count_1 = counts[2 * guest_1 + plan[1, guest_1]]

    pl.semaphore_wait(barrier, 3)

    @pl.when(core == 0)
    def _():
        pl.semaphore_signal(ready, inc=1, device_id=(next_2, 1 - g), device_id_type=mesh_id)

    for k in range(chunks):
        load(k).wait()
        here = rows_of(k)
        first, second = staged[0, here], staged[1, here]
        played_0[here, :] = jnp.where(slot_0 == 0, first, second)
        played_1[here, :] = jnp.where(slot_1 == 0, first, second)

        @pl.when(core == 0)
        def _():
            to_mate_a0(k).start()
            to_core(k).start()

        @pl.when(core == 1)
        def _():
            to_next_b(k).start()

    for k in range(chunks):

        @pl.when(core == 0)
        def _():
            to_mate_b(k).start()

        @pl.when(core == 1)
        def _():
            to_next_a(k).start()

    @pl.when(core == 0)
    def _():
        pl.semaphore_wait(ready, 1)
        for early in range(ahead):
            to_back_a(early).start()

    pair = 2 * chunk
    turn_gate, back_gate = chunks - 3, chunks - 5

    def pair_of(i):
        return pl.ds(pl.multiple_of(i * pair, pair), pair)

    def put_norms(place, source, first, first_row, count, many=2):
        for k in range(many):
            rows = source[rows_of(first + k), :]
            norms[place, pl.ds(first + k, 1), :] = lane_norms(rows, first_row + (first + k) * chunk, count)

    def put_sums(place, first, values):
        for k in range(values.shape[1] // 128):
            sums[place, pl.ds(first + k, 1), :] = values[:, k * 128 : (k + 1) * 128]

    def arrive(stream, first, many=2):
        for k in range(many):
            stream(first + k).wait_recv()

    def own_norms(k, carry):
        put_norms(0, played_0, k, own_row, count_0, 1)
        put_norms(1, played_1, k, own_row, count_1, 1)
        turned_1[:, rows_of(k)] = played_1[rows_of(k), :].T
        return carry

    lax.fori_loop(0, chunks, own_norms, 0)

    def whole(rows, beside, resident, place):
        return tile_sums(rows, beside, resident, norms.at[place], totals.at[place])

    def whole_turned(rows, beside, resident, place):
        return tile_sums(rows, beside, resident, norms.at[place], totals.at[place], True)

    def store(density_0, density_1):
        places = lax.broadcasted_iota(jnp.int32, (chunks, 128), 0) * 128 + lax.broadcasted_iota(jnp.int32, (chunks, 128), 1)
        for slot in range(2):
            both = jnp.where(slot_0 == slot, density_0, 0.0) + jnp.where(slot_1 == slot, density_1, 0.0)
            both = jnp.where(own_row + places < counts[2 * m + slot], both, 0.0)
            for k in range(chunks):
                out[slot : slot + 1, k * 128 : (k + 1) * 128] = both[k : k + 1, :]

    @pl.when(core == 0)
    def _():
        def guests_of_round_0(i, carry):
            for k in range(2):
                to_mate_a0(2 * i + k).wait_recv()
                to_core_passed(2 * i + k).start()

            @pl.when(i == chunks // 2 - 1)
            def _():
                to_back_a(ahead).start()

            arrive(to_next_b, 2 * i)
            put_norms(2, guest_b, 2 * i, far_row, guest_count_0)
            rows = guest_b[pair_of(i), :]
            beside = column_norms(rows, far_row + i * pair, guest_count_0)
            put_sums(0, 2 * i, whole(rows, beside, played_0, 0))
            return carry

        lax.fori_loop(0, chunks // 2, guests_of_round_0, 0)

        def mates_of_round_0(i, carry):
            rows = mate_a[pair_of(i), :]
            beside = column_norms(rows, far_row + i * pair, count_0)
            put_sums(2, 2 * i, whole(rows, beside, guest_b, 2))
            return carry

        lax.fori_loop(0, chunks // 2, mates_of_round_0, 0)
        sums[0] += folded_rows(totals[2])
        sum_copy(0, 5, (back_1, 1 - g)).start()
        sum_copy(2, 0, mate).start()

        def mates_of_round_1(k, carry):
            to_mate_b(k).wait_recv()

            @pl.when(k == turn_gate)
            def _():
                pl.semaphore_signal(turn, inc=1, device_id=other_core, device_id_type=mesh_id)

            @pl.when(k == back_gate)
            def _():
                for late in range(ahead + 1, chunks):
                    to_back_a(late).start()

            put_norms(3, mate_b, k, far_row, count_1, 1)
            turned_mate[:, rows_of(k)] = mate_b[rows_of(k), :].T
            return carry

        lax.fori_loop(0, chunks, mates_of_round_1, 0)

        def guests_of_round_1(first, many):
            arrive(to_back_a, first, many)
            rows = guest_a[pl.ds(pl.multiple_of(first * chunk, chunk), many * chunk), :]
            beside = column_norms(rows, far_row + first * chunk, guest_count_1)
            put_sums(1, first, whole_turned(rows, beside, turned_1, 1) + whole_turned(rows, beside, turned_mate, 3))

        def two_chunks(i, carry):
            guests_of_round_1(2 * i, 2)
            return carry

        lax.fori_loop(0, chunks // 2 - 1, two_chunks, 0)
        for k in range(chunks):
            for sent in (to_mate_a0, to_core, to_core_passed):
                sent(k).wait_send()
        for target in (0, 2, 3):
            sum_copy(0, target, mate).wait_recv()
        density_0 = folded_rows(totals[0]) + arrived[0] + arrived[2] + arrived[3]
        guests_of_round_1(chunks - 2, 1)
        to_back_a(chunks - 1).wait_recv()
        rows = guest_a[half_rows - chunk : half_rows, :]
        beside = column_norms(rows, far_row + half_rows - chunk, guest_count_1)
        far = whole_turned(rows, beside, turned_mate, 3)
        sums[3] = folded_rows(totals[3])
        sum_copy(3, 1, mate).start()
        put_sums(1, chunks - 1, far + whole_turned(rows, beside, turned_1, 1))
        sum_copy(1, 4, (next_2, 1 - g)).start()

        density_1 = folded_rows(totals[1])
        for k in range(chunks):
            for sent in (to_back_a, to_mate_b):
                sent(k).wait_send()
        for source, target in ((0, 5), (2, 0), (3, 1), (1, 4)):
            sum_copy(source, target, mate).wait_send()
        for target in (1, 4):
            sum_copy(0, target, mate).wait_recv()
        store(density_0, density_1 + arrived[1] + arrived[4])

    @pl.when(core == 1)
    def _():
        def near_half(i, carry):
            arrive(to_core, 2 * i)
            rows = chip_guest[0, pair_of(i), :]
            beside = column_norms(rows, own_row + i * pair, guest_count_0)
            put_sums(0, 2 * i, whole(rows, beside, played_0, 0))
            return carry

        lax.fori_loop(0, chunks // 2, near_half, 0)
        sum_copy(0, 2, other_core).start()

        def far_half(i, carry):
            arrive(to_core_passed, 2 * i)
            rows = chip_guest[1, pair_of(i), :]
            beside = column_norms(rows, far_row + i * pair, guest_count_0)
            put_sums(1, 2 * i, whole(rows, beside, played_0, 0))
            return carry

        lax.fori_loop(0, chunks // 2, far_half, 0)
        sum_copy(1, 3, (back_1, 1 - g)).start()

        pl.semaphore_wait(turn, 1)
        for k in range(chunks):
            to_mate_a1(k).start()

        early_rows = half_rows - pair

        def guests_of_round_1(i, carry):
            arrive(to_next_a, 2 * i)
            put_norms(2, guest_a, 2 * i, far_row, guest_count_1)
            rows = guest_a[pair_of(i), :]
            beside = column_norms(rows, far_row + i * pair, guest_count_1)
            put_sums(2, 2 * i, whole(rows, beside, played_1, 1))
            return carry

        lax.fori_loop(0, chunks // 2 - 1, guests_of_round_1, 0)

        def mates_of_round_1(first, many):
            arrive(to_mate_a1, first, many)
            put_norms(3, mate_a, first, far_row, count_1, many)
            for k in range(many):
                turned_mate[:, rows_of(first + k)] = mate_a[rows_of(first + k), :].T
            rows = mate_a[pl.ds(pl.multiple_of(first * chunk, chunk), many * chunk), :]
            beside = column_norms(rows, far_row + first * chunk, count_1)
            put_sums(3, first, whole(rows, beside, guest_a.at[pl.ds(0, early_rows)], 2))

        def two_chunks(i, carry):
            mates_of_round_1(2 * i, 2)
            return carry

        lax.fori_loop(0, chunks // 2 - 1, two_chunks, 0)
        sum_copy(0, 5, mate).wait_recv()
        density_0 = folded_rows(totals[0]) + arrived[5]
        for k in range(chunks):
            to_next_b(k).wait_send()
        mates_of_round_1(chunks - 2, 1)

        def last_guests(k):
            to_next_a(k).wait_recv()
            rows = guest_a[k * chunk : (k + 1) * chunk, :]
            beside = column_norms(rows, far_row + k * chunk, guest_count_1)
            return rows, beside, whole_turned(rows, beside, turned_1, 1)

        rows, beside, near = last_guests(chunks - 2)
        mates_of_round_1(chunks - 1, 1)
        put_sums(2, chunks - 2, near + whole_turned(rows, beside, turned_mate, 3))
        rows, beside, near = last_guests(chunks - 1)
        put_sums(2, chunks - 1, near + whole_turned(rows, beside, turned_mate, 3))
        sums[2] += folded_rows(totals[2])
        sum_copy(2, 4, (back_2, 1 - g)).start()
        sums[3] += folded_rows(totals[3])
        sum_copy(3, 1, mate).start()
        density_1 = folded_rows(totals[1])
        for k in range(chunks):
            for sent in (to_next_a, to_mate_a1):
                sent(k).wait_send()
        for source, target in ((0, 2), (1, 3), (2, 4), (3, 1)):
            sum_copy(source, target, mate).wait_send()
        for target in (1, 4):
            sum_copy(0, target, mate).wait_recv()
        store(density_0, density_1 + arrived[1] + arrived[4])


def on_device(embeddings, counts, plan):
    _, half_rows, width = embeddings.shape
    chunks = half_rows // chunk
    half_block = pltpu.VMEM((half_rows, width), embeddings.dtype)
    turned_block = pltpu.VMEM((width, half_rows), embeddings.dtype)
    two_halves = pltpu.VMEM((2, half_rows, width), embeddings.dtype)
    return pl.pallas_call(
        functools.partial(kernel, lax.axis_size("blk")),
        out_shape=jax.ShapeDtypeStruct((2, half_rows), jnp.float32),
        in_specs=[
            pl.BlockSpec(memory_space=pltpu.HBM),
            pl.BlockSpec(memory_space=pltpu.HBM),
            pl.BlockSpec(memory_space=pltpu.HBM),
        ],
        out_specs=pl.BlockSpec(memory_space=pltpu.VMEM),
        scratch_shapes=[
            pltpu.SMEM(plan.shape[::-1], plan.dtype),
            pltpu.SMEM(counts.shape, counts.dtype),
            two_halves,
            half_block, half_block, half_block, half_block, half_block, half_block,
            two_halves,
            turned_block, turned_block,
            pltpu.VMEM((4, chunks, 128), jnp.float32),
            pltpu.VMEM((4, 8, half_rows), jnp.float32),
            pltpu.VMEM((4, chunks, 128), jnp.float32),
            pltpu.VMEM((6, chunks, 128), jnp.float32),
            pltpu.SemaphoreType.REGULAR,
            pltpu.SemaphoreType.REGULAR,
            pltpu.SemaphoreType.DMA((2,)),
            pltpu.SemaphoreType.DMA((chunks,)),
            pltpu.SemaphoreType.DMA((6, chunks)),
            pltpu.SemaphoreType.DMA((6, chunks)),
            pltpu.SemaphoreType.DMA((6,)),
            pltpu.SemaphoreType.DMA((6,)),
        ],
        compiler_params=pltpu.CompilerParams(
            collective_id=0, has_side_effects=True, vmem_limit_bytes=32 * 2**20
        ),
    )(*(pltpu.with_memory_space_constraint(operand, pltpu.HBM) for operand in (plan.T, counts, embeddings)))


def solution(mesh):
    return jax.shard_map(
        on_device,
        mesh=mesh,
        in_specs=(P("blk", "grp", None), P(), P()),
        out_specs=P("blk", "grp"),
        check_vma=False,
    )
```
